256 devices in a mesh: dp: 32 (over x_hi, z, core), seq: 8 (over y, x_lo).
Axes of the slice: x: 4 (x_hi: 2, x_lo: 2; x = x_hi * 2 + x_lo), y: 4, z: 8, core: 2. Of those that a mesh axis runs over, the one named last changes fastest.
Arguments:
- inputs: bfloat16 [32, 1024, 1536], P('dp', 'seq'), may hold values from -6 to 6
- saved: bfloat16 [32, 1024, 1536], P('dp', 'seq'), may hold values from -32 to 32
- attn_saved: bfloat16 [32, 1024, 1536], P('dp', 'seq'), may hold values from -6 to 6
- upstream: bfloat16 [32, 1024, 1536], P('dp', 'seq'), may hold values from -6 to 6
- w_qkv: bfloat16 [1536, 3, 1536], P(None, None, 'seq'), may hold values from -0.15625 to 0.15625
- w_out: bfloat16 [1536, 1536], P('seq'), may hold values from -0.15625 to 0.15625
- w_conv: bfloat16 [5, 1536, 1536], P(None, ('seq', 'dp')), may hold values from -0.0625 to 0.0625
Outputs:
- grad_inputs: bfloat16 [32, 1024, 1536], P('dp', 'seq')
- grad_qkv: bfloat16 [1536, 3, 1536], P('dp', None, 'seq')
- grad_out: bfloat16 [1536, 1536], P(('seq', 'dp'))
- grad_conv: bfloat16 [5, 1536, 1536], P(None, ('seq', 'dp'))
The draws below stay inside these ranges and needn't reach their ends.
All inputs are finite; a program needn't handle non-finite values.
Results may differ from the reference program's by a relative error of at most 0.034.
Values may be sent and summed in bfloat16 or wider, within the bound.
A program may use at most 128 MiB of HBM per device.

```python
import math
import jax
import jax.numpy as jnp
from jax import lax

C = 1536
HEADS = 8
HD = 192
TAPS = 5
DILATION = 32
L = 1024
BATCH = 32


def draw_saved(key, part):
    key = jax.random.fold_in(key, 3)
    first_key, second_key, third_key = jax.random.split(key, 3)
    base_draw = jnp.clip(jax.random.normal(first_key, (BATCH, L, C), jnp.float32), -5.0, 5.0)
    row_scale = jnp.exp(jax.random.uniform(second_key, (BATCH, L, 1), jnp.float32, 0.0, math.log(10.0)))
    col_scale = jnp.exp(jax.random.uniform(third_key, (1, 1, C), jnp.float32, 0.0, math.log(10.0)))
    return (0.0625 * base_draw * row_scale * col_scale).astype(jnp.bfloat16)


def level_of(key, extent, cuts, low, top_value):
    def one(dim, shards_of):
        draws = jax.random.uniform(jax.random.fold_in(jax.random.fold_in(key, 6), dim), (shards_of,), jnp.float32, low / len(cuts), top_value / len(cuts))
        return jnp.repeat(jnp.exp(draws), extent[dim] // shards_of).reshape((-1,) + (1,) * (len(extent) - dim - 1))

    factor_of = one(*cuts[0])
    for cut in cuts[1:]:
        factor_of = factor_of * one(*cut)
    return factor_of


def gaussian(key, dims, deviation, limit, cuts=(), dtype=jnp.bfloat16):
    entries = deviation * jax.random.normal(key, dims, jnp.float32)
    if cuts:
        entries = entries * level_of(key, dims, cuts, -0.22, 0.18)
    return jnp.clip(entries, -limit, limit).astype(dtype)


def setup_inputs(seed: int = 0) -> dict:
    keys = jax.random.split(jax.random.key(seed), 8)
    return {
        "inputs": gaussian(keys[0], (BATCH, L, C), 1.0, 6.0, ((0, 32), (1, 8))),
        "saved": draw_saved(jax.random.fold_in(keys[7], 71), 0),
        "attn_saved": gaussian(keys[2], (BATCH, L, C), 1.0, 6.0, ((0, 32), (1, 8))),
        "upstream": gaussian(keys[3], (BATCH, L, C), 1.0, 6.0, ((0, 32), (1, 8))),
        "w_qkv": gaussian(keys[4], (C, 3, C), C ** -0.5, 0.15625, ((2, 8),)),
        "w_out": gaussian(keys[5], (C, C), C ** -0.5, 0.15625, ((0, 8),)),
        "w_conv": gaussian(keys[6], (TAPS, C, C), (TAPS * C) ** -0.5, 0.0625, ((1, 256),)),
    }


EPSILON = 1e-06

def to_half(values):
    return lax.optimization_barrier(values.astype(jnp.bfloat16))

def gelu_slope(values):
    return jax.jvp(jax.nn.gelu, (values,), (jnp.ones_like(values),))[1]

def one_sequence(inputs, saved, attn_saved, upstream, w_qkv, w_out, w_conv):
    saved_wide = saved.astype(jnp.float32)
    inverse = lax.rsqrt(lax.optimization_barrier(jnp.mean(saved_wide * saved_wide, axis=-1, keepdims=True)) + EPSILON)
    normed = saved_wide * inverse
    normed_half = to_half(normed)
    projected = to_half(jnp.dot(normed_half, w_qkv.reshape(C, 3 * C), preferred_element_type=jnp.float32))
    projected = projected.astype(jnp.float32).reshape(L, 3, HEADS, HD)
    queries = projected[:, 0]
    keys_all = projected[:, 1]
    values_all = projected[:, 2]
    grad_attn = to_half(jnp.dot(upstream, w_out.T, preferred_element_type=jnp.float32))
    grad_attn = grad_attn.astype(jnp.float32).reshape(L, HEADS, HD)
    score_scale = HD ** (-0.5)
    scores = jnp.einsum('qhd,khd->hqk', queries, keys_all) * score_scale
    exponent = jnp.exp(scores)
    attn_probs = exponent / lax.optimization_barrier(jnp.sum(exponent, axis=-1, keepdims=True))
    probs_half = to_half(attn_probs).astype(jnp.float32)
    attn_wide = attn_saved.astype(jnp.float32).reshape(L, HEADS, HD)
    row_delta = jnp.einsum('qhd,qhd->hq', grad_attn, attn_wide)[:, :, None]
    grad_prob = jnp.einsum('qhd,khd->hqk', grad_attn, values_all)
    grad_score = to_half(attn_probs * (grad_prob - row_delta) * score_scale).astype(jnp.float32)
    grad_query = to_half(jnp.einsum('hqk,khd->qhd', grad_score, keys_all))
    grad_key = to_half(jnp.einsum('hqk,qhd->khd', grad_score, queries))
    grad_value = to_half(jnp.einsum('hqk,qhd->khd', probs_half, grad_attn))
    grad_proj = jnp.stack([grad_query, grad_key, grad_value], axis=1).reshape(L, 3 * C)
    seq_qkv = jnp.dot(normed_half.T, grad_proj, preferred_element_type=jnp.float32).reshape(C, 3, C)
    seq_out = jnp.dot(attn_saved.T, upstream, preferred_element_type=jnp.float32)
    grad_acts = jnp.dot(grad_proj, w_qkv.reshape(C, 3 * C).T, preferred_element_type=jnp.float32)
    grad_saved = inverse * (grad_acts - normed * lax.optimization_barrier(jnp.mean(grad_acts * normed, axis=-1, keepdims=True)))
    grad_mid = to_half(upstream.astype(jnp.float32) + grad_saved)
    gelu_out = jax.nn.gelu(inputs.astype(jnp.float32)).astype(jnp.bfloat16)
    conv_reach = DILATION * (TAPS // 2)
    gelu_pad = jnp.pad(gelu_out, ((conv_reach, conv_reach), (0, 0)))
    mid_pad = jnp.pad(grad_mid, ((conv_reach, conv_reach), (0, 0)))
    seq_conv = jnp.stack([jnp.dot(gelu_pad[DILATION * tap_index:DILATION * tap_index + L].T, grad_mid, preferred_element_type=jnp.float32) for tap_index in range(TAPS)])
    grad_gelu = jnp.zeros((L, C), jnp.float32)
    for tap_index in range(TAPS):
        offset = 2 * conv_reach - DILATION * tap_index
        grad_gelu = grad_gelu + jnp.dot(mid_pad[offset:offset + L], w_conv[tap_index].T, preferred_element_type=jnp.float32)
    grad_gelu = to_half(grad_gelu).astype(jnp.float32)
    grad_rows = (grad_mid.astype(jnp.float32) + gelu_slope(inputs.astype(jnp.float32)) * grad_gelu).astype(jnp.bfloat16)
    return (grad_rows, seq_qkv, seq_out, seq_conv)

def reference(inputs, saved, attn_saved, upstream, w_qkv, w_out, w_conv):

    def per_sequence(totals, sequence):
        grad_rows, seq_qkv, seq_out, seq_conv = one_sequence(sequence[0], sequence[1], sequence[2], sequence[3], w_qkv, w_out, w_conv)
        updated = (totals[0] + to_half(seq_qkv).astype(jnp.float32), totals[1] + to_half(seq_out).astype(jnp.float32), totals[2] + to_half(seq_conv).astype(jnp.float32))
        return (updated, grad_rows)
    zero_totals = (jnp.zeros((C, 3, C), jnp.float32), jnp.zeros((C, C), jnp.float32), jnp.zeros((TAPS, C, C), jnp.float32))
    totals, grad_inputs = lax.scan(per_sequence, zero_totals, (inputs, saved, attn_saved, upstream))
    return (grad_inputs, totals[0].astype(jnp.bfloat16), totals[1].astype(jnp.bfloat16), totals[2].astype(jnp.bfloat16))
```

```python
import jax
import jax.numpy as jnp
from jax import lax
from jax.experimental import pallas as pl
from jax.experimental.pallas import tpu as pltpu
from jax.sharding import PartitionSpec as P

HD = 192
TAPS = 5
DILATION = 32
EPSILON = 1e-06
REACH = DILATION * (TAPS // 2)
BF16 = jnp.bfloat16
F32 = jnp.float32
MESH = pl.DeviceIdType.MESH
VMEM = pltpu.VMEM
ANY = pl.ANY


def gelu_slope(values):
    return jax.jvp(jax.nn.gelu, (values,), (jnp.ones_like(values),))[1]


def seq_at(dy, dx):
    here = lax.axis_index("seq")
    return lax.rem(here // 2 + dy, 4) * 2 + lax.rem(here + dx, 2)


def dp_at(dxh, dz, dcore):
    here = lax.axis_index("dp")
    core = lax.rem(here + dcore, 2)
    z = lax.rem(here // 2 + dz, 8)
    xh = lax.rem(here // 16 + dxh, 2)
    return (xh * 8 + z) * 2 + core


SEQ_OFFSETS = [(dy, dx) for dy in (2, 1, 3, 0) for dx in (1, 0) if (dy, dx) != (0, 0)]


def meet(peers):
    barrier = pltpu.get_barrier_semaphore()
    for peer in peers:
        pl.semaphore_signal(barrier, inc=1, device_id=peer, device_id_type=MESH)
    pl.semaphore_wait(barrier, len(peers))


class Wires:
    def __init__(self, send_sems, recv_sems):
        self.send_sems, self.recv_sems = send_sems, recv_sems
        self.used = 0
        self.copies = []

    def send(self, source, target, device):
        copy = pltpu.make_async_remote_copy(
            source,
            target,
            self.send_sems.at[self.used],
            self.recv_sems.at[self.used],
            device_id=device,
            device_id_type=MESH,
        )
        copy.start()
        self.used += 1
        self.copies.append(copy)
        return copy

    def finish(self):
        for copy in self.copies:
            copy.wait_send()


def gather_steps(wires, source, whole):
    up, down, across = {"seq": seq_at(1, 0)}, {"seq": seq_at(3, 0)}, {"seq": seq_at(0, 1)}
    here = lax.axis_index("seq")
    half = source.shape[0] // 2
    state = {}

    def first():
        state["up"] = wires.send(source, whole.at[here], up)
        state["down"] = wires.send(source, whole.at[here], down)
        state["across"] = wires.send(source, whole.at[here], across)

    def second():
        state["up"].wait_recv()
        part = whole.at[seq_at(3, 0), pl.ds(0, half)]
        state["far_up"] = wires.send(part, part, up)
        state["down"].wait_recv()
        part = whole.at[seq_at(1, 0), pl.ds(half, half)]
        state["far_down"] = wires.send(part, part, down)
        part = whole.at[seq_at(1, 0)]
        state["over"] = wires.send(part, part, across)
        state["across"].wait_recv()
        part = whole.at[seq_at(0, 1)]
        state["side_up"] = wires.send(part, part, up)

    def third():
        state["over"].wait_recv()
        part = whole.at[seq_at(1, 1)]
        state["side_down"] = wires.send(part, part, down)

    def last():
        for name in ("far_up", "far_down", "side_up", "side_down"):
            state[name].wait_recv()

    return first, second, third, last


GATHER_SENDS = 8


def scatter_steps(wires, parts, inbox):
    up, down, across = {"seq": seq_at(1, 0)}, {"seq": seq_at(3, 0)}, {"seq": seq_at(0, 1)}
    here = lax.axis_index("seq")
    half = parts.shape[1] // 2
    top, bottom = pl.ds(0, half), pl.ds(half, half)
    state = {}

    def first():
        state["c1"] = wires.send(parts.at[seq_at(2, 1)], inbox.at[0], up)
        state["c2"] = wires.send(parts.at[seq_at(3, 1)], inbox.at[1], down)
        far = seq_at(2, 0)
        state["ct"] = wires.send(parts.at[far, top], inbox.at[2, top], down)
        state["cb"] = wires.send(parts.at[far, bottom], inbox.at[2, bottom], up)

    def second():
        state["c1"].wait_recv()
        inbox[0] = inbox[0] + parts[seq_at(1, 1)]
        state["c4"] = wires.send(inbox.at[0], inbox.at[3], across)
        state["c2"].wait_recv()
        inbox[1] = inbox[1] + parts[seq_at(0, 1)]
        state["c5"] = wires.send(inbox.at[1], inbox.at[4], across)
        to = seq_at(3, 0)
        state["c6b"] = wires.send(parts.at[to, bottom], inbox.at[5, bottom], down)
        state["ct"].wait_recv()
        inbox[2, top] = inbox[2, top] + parts[to, top]
        state["c6t"] = wires.send(inbox.at[2, top], inbox.at[5, top], down)

    def third():
        state["cb"].wait_recv()
        state["c4"].wait_recv()
        to = seq_at(1, 0)
        inbox[3] = (parts[to].astype(F32) + inbox[3].astype(F32)).astype(BF16)
        inbox[3, bottom] = inbox[3, bottom] + inbox[2, bottom]
        state["c7"] = wires.send(inbox.at[3], inbox.at[6], up)

    def last():
        for name in ("c5", "c6b", "c6t", "c7"):
            state[name].wait_recv()
        return (parts[here].astype(F32) + inbox[4].astype(F32)) + (
            inbox[5].astype(F32) + inbox[6].astype(F32)
        )

    return first, second, third, last


SCATTER_SENDS = 9


def total_steps(wires, terms, acc, above, below, beside, out):
    core = lax.rem(lax.axis_index("dp"), 2)
    z = lax.rem(lax.axis_index("dp") // 2, 8)
    xh = lax.axis_index("dp") // 16
    twin, up, down = {"dp": dp_at(0, 0, 1)}, {"dp": dp_at(0, 1, 0)}, {"dp": dp_at(0, 7, 0)}
    far = {"dp": dp_at(1, 0, 0)}
    state = {}

    def at(dz):
        return lax.rem(z + dz, 8)

    def start():
        state["twin"] = wires.send(terms.at[:, 1 - core], acc, twin)

    def first():
        state["twin"].wait_recv()
        chips = terms.shape[0]

        @pl.loop(0, chips)
        def _(chip):
            acc[chip] = acc[chip] + terms[chip, core]

        state["u"] = wires.send(acc.at[at(4)], above.at[0, 0], up)
        state["d"] = wires.send(acc.at[8 + at(4)], below.at[0, 1], down)

    def middle(step):
        def run():
            to_up, to_down = at(4 - step), at(4 + step)
            state["u"].wait_recv()
            acc[to_up] = acc[to_up] + above[step - 1, 0]
            if step > 1:
                acc[8 + to_up] = acc[8 + to_up] + above[step - 1, 1]
            state["u0"] = wires.send(acc.at[to_up], above.at[step, 0], up)
            state["u1"] = wires.send(acc.at[8 + to_up], above.at[step, 1], up)
            state["d"].wait_recv()
            acc[8 + to_down] = acc[8 + to_down] + below[step - 1, 1]
            if step > 1:
                acc[to_down] = acc[to_down] + below[step - 1, 0]
            state["d0"] = wires.send(acc.at[to_down], below.at[step, 0], down)
            state["d1"] = wires.send(acc.at[8 + to_down], below.at[step, 1], down)
            state["u"], state["d"] = Both(state["u0"], state["u1"]), Both(state["d0"], state["d1"])

        return run

    def cross():
        state["u"].wait_recv()
        state["d"].wait_recv()
        other = 1 - xh
        to = other * 8 + z
        acc[to] = (
            acc[to].astype(F32) + above[3, other].astype(F32) + below[3, other].astype(F32)
        ).astype(BF16)
        state["far"] = wires.send(acc.at[to], beside, far)

    def last():
        state["far"].wait_recv()
        total = acc[xh * 8 + z].astype(F32) + above[3, xh].astype(F32)
        out[...] = (total + below[3, xh].astype(F32) + beside[...].astype(F32)).astype(BF16)

    return start, first, middle(1), middle(2), middle(3), cross, last


TOTAL_SENDS = 1 + 2 + 3 * 4 + 1


class Both:
    def __init__(self, *copies):
        self.copies = copies

    def wait_recv(self):
        for copy in self.copies:
            copy.wait_recv()


def total_scratch(rows, columns):
    return [
        VMEM((16, rows, columns), BF16),
        VMEM((4, 2, rows, columns), BF16),
        VMEM((4, 2, rows, columns), BF16),
        VMEM((rows, columns), BF16),
    ]


def sems(count):
    return [pltpu.SemaphoreType.DMA((count,)), pltpu.SemaphoreType.DMA((count,))]


def params(collective_id):
    return pltpu.CompilerParams(
        collective_id=collective_id, has_side_effects=True, vmem_limit_bytes=48 << 20
    )


def gather_kernel(saved, upstream, gelu, attn, saved_all, upstream_all, gelu_all, attn_all, *scratch):
    own, send_sems, recv_sems = scratch
    here = lax.axis_index("seq")
    meet([{"seq": seq_at(*offset)} for offset in SEQ_OFFSETS])
    wires = Wires(send_sems, recv_sems)
    locals_ = [
        (saved, saved_all.at[here]),
        (upstream, upstream_all.at[here]),
        (gelu.at[here], gelu_all.at[here]),
        (attn.at[here], attn_all.at[here]),
    ]
    kept = [pltpu.make_async_copy(a, b, own.at[i]) for i, (a, b) in enumerate(locals_)]
    for copy in kept:
        copy.start()
    pairs = [gather_steps(wires, saved, saved_all), gather_steps(wires, upstream, upstream_all)]
    swapped = []
    for step in range(3):
        for steps in pairs:
            steps[step]()
        if step == 1:
            for offset in SEQ_OFFSETS:
                to = seq_at(*offset)
                swapped.append(wires.send(attn.at[to], attn_all.at[here], {"seq": to}))
                swapped.append(wires.send(gelu.at[to], gelu_all.at[here], {"seq": to}))
    for steps in pairs:
        steps[3]()
    for copy in swapped:
        copy.wait_recv()
    wires.finish()
    for copy in kept:
        copy.wait()


def gather(saved, upstream, gelu, attn):
    count = 2 * GATHER_SENDS + 2 * 7
    blocks = (8,) + saved.shape
    return pl.pallas_call(
        gather_kernel,
        out_shape=[
            jax.ShapeDtypeStruct(blocks, BF16),
            jax.ShapeDtypeStruct(blocks, BF16),
            jax.ShapeDtypeStruct(gelu.shape, BF16),
            jax.ShapeDtypeStruct(attn.shape, BF16),
        ],
        in_specs=[pl.BlockSpec(memory_space=ANY)] * 4,
        out_specs=[pl.BlockSpec(memory_space=ANY)] * 4,
        scratch_shapes=[pltpu.SemaphoreType.DMA((4,))] + sems(count),
        compiler_params=params(1),
    )(saved, upstream, gelu, attn)


def middle_kernel(parts, saved, upstream, qkv, outs, mid_all, qkv_sum, out_sum, *scratch):
    inbox, mine = scratch[:2]
    qkv_bufs, out_bufs = scratch[2:6], scratch[6:10]
    send_sems, recv_sems, own = scratch[10:]
    here = lax.axis_index("seq")
    meet(
        [{"seq": seq_at(*offset)} for offset in ((1, 0), (3, 0), (0, 1))]
        + [{"dp": dp_at(*offset)} for offset in ((0, 0, 1), (0, 1, 0), (0, 7, 0), (1, 0, 0))]
    )
    wires = Wires(send_sems, recv_sems)
    scatter = scatter_steps(wires, parts, inbox)
    gather_ = gather_steps(wires, mine, mid_all)
    sums = [
        total_steps(wires, qkv, *qkv_bufs, qkv_sum),
        total_steps(wires, outs, *out_bufs, out_sum),
    ]

    def both(step):
        for steps in sums:
            steps[step]()

    scatter[0]()
    both(0)
    both(1)
    scatter[1]()
    both(2)
    scatter[2]()
    both(3)
    acts = scatter[3]()
    wide = saved[...].astype(F32)
    inverse = lax.rsqrt(jnp.mean(wide * wide, axis=-1, keepdims=True) + EPSILON)
    normed = wide * inverse
    grad = inverse * (acts - normed * jnp.mean(acts * normed, axis=-1, keepdims=True))
    mine[...] = (upstream[...].astype(F32) + grad).astype(BF16)
    gather_[0]()
    kept = pltpu.make_async_copy(mine, mid_all.at[here], own.at[0])
    kept.start()
    both(4)
    gather_[1]()
    both(5)
    gather_[2]()
    both(6)
    gather_[3]()
    wires.finish()
    kept.wait()


def middle(parts, saved, upstream, qkv, outs):
    count = GATHER_SENDS + SCATTER_SENDS + 2 * TOTAL_SENDS
    rows = saved.shape
    qkv_rows, out_rows = qkv.shape[2:], outs.shape[2:]
    return pl.pallas_call(
        middle_kernel,
        out_shape=[
            jax.ShapeDtypeStruct((8,) + rows, BF16),
            jax.ShapeDtypeStruct(qkv_rows, BF16),
            jax.ShapeDtypeStruct(out_rows, BF16),
        ],
        in_specs=[pl.BlockSpec(memory_space=VMEM)] * 5,
        out_specs=[pl.BlockSpec(memory_space=VMEM)] * 3,
        scratch_shapes=[VMEM((7,) + rows, BF16), VMEM(rows, BF16)]
        + total_scratch(*qkv_rows)
        + total_scratch(*out_rows)
        + sems(count)
        + [pltpu.SemaphoreType.DMA((1,))],
        compiler_params=params(2),
    )(parts, saved, upstream, qkv, outs)


def final_kernel(gelu, conv_a, conv_b, gelu_back, sum_a, sum_b, *scratch):
    bufs_a, bufs_b = scratch[:4], scratch[4:8]
    send_sems, recv_sems, own = scratch[8:]
    here = lax.axis_index("seq")
    meet(
        [{"seq": seq_at(*offset)} for offset in SEQ_OFFSETS]
        + [{"dp": dp_at(*offset)} for offset in ((0, 0, 1), (0, 1, 0), (0, 7, 0), (1, 0, 0))]
    )
    wires = Wires(send_sems, recv_sems)
    sums = [
        total_steps(wires, conv_a, *bufs_a, sum_a),
        total_steps(wires, conv_b, *bufs_b, sum_b),
    ]
    for steps in sums:
        steps[0]()
    swapped = []
    for offset in SEQ_OFFSETS:
        to = seq_at(*offset)
        swapped.append(wires.send(gelu.at[to], gelu_back.at[here], {"seq": to}))
    kept = pltpu.make_async_copy(gelu.at[here], gelu_back.at[here], own.at[0])
    kept.start()
    for step in range(1, 7):
        for steps in sums:
            steps[step]()
    for copy in swapped:
        copy.wait_recv()
    wires.finish()
    kept.wait()


def final(gelu, conv_a, conv_b):
    count = 7 + 2 * TOTAL_SENDS
    rows = conv_a.shape[2:]
    return pl.pallas_call(
        final_kernel,
        out_shape=[
            jax.ShapeDtypeStruct(gelu.shape, BF16),
            jax.ShapeDtypeStruct(rows, BF16),
            jax.ShapeDtypeStruct(rows, BF16),
        ],
        in_specs=[pl.BlockSpec(memory_space=VMEM)] * 3,
        out_specs=[pl.BlockSpec(memory_space=VMEM)] * 3,
        scratch_shapes=total_scratch(*rows)
        + total_scratch(*rows)
        + sems(count)
        + [pltpu.SemaphoreType.DMA((1,))],
        compiler_params=params(3),
    )(gelu, conv_a, conv_b)


def spread(rows, group, slots, offset):
    source = lax.broadcasted_iota(jnp.int32, (rows, rows // group * slots), 0)
    target = lax.broadcasted_iota(jnp.int32, (rows, rows // group * slots), 1)
    return (source // group * slots + offset + source % group == target).astype(BF16)


def shifted(array, rows):
    if rows == 0:
        return array
    zeros = jnp.zeros((abs(rows), array.shape[1]), array.dtype)
    if rows > 0:
        return jnp.concatenate([array[rows:], zeros])
    return jnp.concatenate([zeros, array[:rows]])


def dot(a, b, dims, out=F32):
    return lax.dot_general(a, b, (dims, ((), ())), preferred_element_type=F32).astype(out)


def local(inputs, saved, attn_saved, upstream, w_qkv, w_out, w_conv):
    rows_here, channels = inputs.shape[1:]
    head_width = w_qkv.shape[2]
    taps_rows = w_conv.shape[0] * w_conv.shape[1]
    input_rows = inputs[0]
    saved_rows, upstream_rows = saved[0], upstream[0]

    def head_blocks(array):
        return array.reshape(rows_here, 8, head_width).transpose(1, 0, 2)

    gelu_rows = jax.nn.gelu(input_rows.astype(F32)).astype(BF16)
    conv_block = jnp.pad(w_conv.reshape(taps_rows, channels), ((0, 32 - taps_rows), (0, 0)))
    conv_blocks = lax.all_gather(conv_block, "dp", axis=0, tiled=True)
    saved_all, upstream_all, gelu_cols, attn_cols = gather(
        saved_rows, upstream_rows, head_blocks(gelu_rows), head_blocks(attn_saved[0])
    )
    seq_len = 8 * rows_here
    saved_all = saved_all.reshape(seq_len, channels)
    upstream_all = upstream_all.reshape(seq_len, channels)
    gelu_cols = gelu_cols.reshape(seq_len, head_width)
    attn_cols = attn_cols.reshape(seq_len, head_width)

    wide = saved_all.astype(F32)
    inverse = lax.rsqrt(jnp.mean(wide * wide, axis=-1, keepdims=True) + EPSILON)
    normed_half = (wide * inverse).astype(BF16)
    w_flat = w_qkv.reshape(channels, 3 * head_width)
    projected = dot(normed_half, w_flat, ((1,), (0,)), BF16)
    queries, keys_all, values_all = jnp.split(projected, 3, axis=1)
    grad_attn = dot(upstream_all, w_out, ((1,), (1,)), BF16)
    row_delta = jnp.sum(grad_attn.astype(F32) * attn_cols.astype(F32), axis=1, keepdims=True)
    scale = HD ** (-0.5)
    scores = dot(queries, keys_all, ((1,), (1,))) * scale
    exponent = jnp.exp(scores)
    probs = exponent / jnp.sum(exponent, axis=-1, keepdims=True)
    grad_prob = dot(grad_attn, values_all, ((1,), (1,)))
    grad_score = (probs * (grad_prob - row_delta) * scale).astype(BF16)
    grad_query = dot(grad_score, keys_all, ((1,), (0,)), BF16)
    grad_key = dot(grad_score, queries, ((0,), (0,)), BF16)
    grad_value = dot(probs.astype(BF16), grad_attn, ((0,), (0,)), BF16)
    grad_proj = jnp.concatenate([grad_query, grad_key, grad_value], axis=1)

    grad_acts = dot(grad_proj, w_flat, ((1,), (1,)), BF16)
    seq_qkv = dot(normed_half, grad_proj, ((0,), (0,)), BF16)
    rows_out = head_width // 32
    seq_out = sum(
        dot(
            dot(attn_cols, spread(head_width, rows_out, 16, rows_out * part), ((1,), (0,)), BF16),
            upstream_all[:, part * channels // 2 : (part + 1) * channels // 2],
            ((0,), (0,)),
        )
        for part in range(2)
    ).astype(BF16)
    mid_all, qkv_sum, out_sum = middle(
        grad_acts.reshape(8, rows_here, channels),
        saved_rows,
        upstream_rows,
        seq_qkv.reshape(16, 2, channels // 32, 3 * head_width),
        seq_out.reshape(16, 2, 16, channels // 2),
    )
    mid_rows = lax.dynamic_index_in_dim(mid_all, lax.axis_index("seq"), 0, False)
    mid_all = mid_all.reshape(seq_len, channels)

    rows_conv = w_conv.shape[1]
    gelu_taps = sum(
        dot(
            shifted(gelu_cols, DILATION * tap - REACH),
            spread(head_width, rows_conv, 32, rows_conv * tap),
            ((1,), (0,)),
        )
        for tap in range(TAPS)
    ).astype(BF16)
    half = channels // 2
    conv_a, conv_b = (
        dot(gelu_taps, mid_all[:, part * half : (part + 1) * half], ((0,), (0,)), BF16)
        for part in range(2)
    )
    grad_gelu = sum(
        dot(
            shifted(mid_all, REACH - DILATION * tap),
            dot(
                spread(head_width, rows_conv, 32, rows_conv * tap),
                conv_blocks,
                ((1,), (0,)),
                BF16,
            ),
            ((1,), (1,)),
        )
        for tap in range(TAPS)
    ).astype(BF16)
    gelu_back, sum_a, sum_b = final(
        grad_gelu.reshape(8, rows_here, head_width),
        conv_a.reshape(16, 2, 32, half),
        conv_b.reshape(16, 2, 32, half),
    )
    grad_gelu_rows = gelu_back.transpose(1, 0, 2).reshape(rows_here, channels)
    grad_rows = (
        mid_rows.astype(F32) + gelu_slope(input_rows.astype(F32)) * grad_gelu_rows.astype(F32)
    ).astype(BF16)
    out_pair = out_sum[: 2 * rows_out].reshape(2, rows_out, half)
    return (
        grad_rows[None],
        qkv_sum.reshape(channels // 32, 3, head_width),
        jnp.concatenate([out_pair[0], out_pair[1]], axis=1),
        jnp.concatenate([sum_a, sum_b], axis=1)[:taps_rows].reshape(w_conv.shape),
    )


def solution(mesh):
    placed = (
        P("dp", "seq", None),
        P("dp", "seq", None),
        P("dp", "seq", None),
        P("dp", "seq", None),
        P(None, None, "seq"),
        P("seq", None),
        P(None, ("seq", "dp"), None),
    )
    return jax.shard_map(
        local,
        mesh=mesh,
        in_specs=placed,
        out_specs=(
            P("dp", "seq", None),
            P("dp", None, "seq"),
            P(("seq", "dp"), None),
            P(None, ("seq", "dp"), None),
        ),
        check_vma=False,
    )
```

```python
import math

import jax
import jax.numpy as jnp
from jax import lax
from jax.experimental import pallas as pl
from jax.experimental.pallas import tpu as pltpu
from jax.sharding import PartitionSpec as P

HD = 192
TAPS = 5
DILATION = 32
EPSILON = 1e-06
REACH = DILATION * (TAPS // 2)
BF16 = jnp.bfloat16
F32 = jnp.float32
MESH = pl.DeviceIdType.MESH
VMEM = pltpu.VMEM
ANY = pl.ANY


def seq_at(dy, dx):
    here = lax.axis_index("seq")
    return lax.rem(here // 2 + dy, 4) * 2 + lax.rem(here + dx, 2)


def dp_at(dxh, dz, dcore):
    here = lax.axis_index("dp")
    core = lax.rem(here + dcore, 2)
    z = lax.rem(here // 2 + dz, 8)
    xh = lax.rem(here // 16 + dxh, 2)
    return (xh * 8 + z) * 2 + core


SEQ_OFFSETS = [(dy, dx) for dy in (2, 1, 3, 0) for dx in (1, 0) if (dy, dx) != (0, 0)]


def meet(peers):
    barrier = pltpu.get_barrier_semaphore()
    for peer in peers:
        pl.semaphore_signal(barrier, inc=1, device_id=peer, device_id_type=MESH)
    pl.semaphore_wait(barrier, len(peers))


class Wires:
    def __init__(self, send_sems, recv_sems):
        self.send_sems, self.recv_sems = send_sems, recv_sems
        self.used = 0
        self.copies = []

    def send(self, source, target, device):
        copy = pltpu.make_async_remote_copy(
            source,
            target,
            self.send_sems.at[self.used],
            self.recv_sems.at[self.used],
            device_id=device,
            device_id_type=MESH,
        )
        copy.start()
        self.used += 1
        self.copies.append(copy)
        return copy

    def finish(self):
        for copy in self.copies:
            copy.wait_send()


def gather_steps(wires, source, place, rows):
    up, down, across = {"seq": seq_at(1, 0)}, {"seq": seq_at(3, 0)}, {"seq": seq_at(0, 1)}
    half = rows // 2
    state = {}

    def first():
        mine = place(lax.axis_index("seq"), 0, rows)
        state["up"] = wires.send(source, mine, up)
        state["down"] = wires.send(source, mine, down)
        state["across"] = wires.send(source, mine, across)

    def second():
        state["up"].wait_recv()
        part = place(seq_at(3, 0), 0, half)
        state["far_up"] = wires.send(part, part, up)
        state["down"].wait_recv()
        part = place(seq_at(1, 0), half, half)
        state["far_down"] = wires.send(part, part, down)
        part = place(seq_at(1, 0), 0, rows)
        state["over"] = wires.send(part, part, across)
        state["across"].wait_recv()
        part = place(seq_at(0, 1), 0, rows)
        state["side_up"] = wires.send(part, part, up)

    def third():
        state["over"].wait_recv()
        part = place(seq_at(1, 1), 0, rows)
        state["side_down"] = wires.send(part, part, down)

    def last():
        for name in ("far_up", "far_down", "side_up", "side_down"):
            state[name].wait_recv()

    return first, second, third, last


GATHER_SENDS = 8


def scatter_steps(wires, parts, inbox):
    up, down, across = {"seq": seq_at(1, 0)}, {"seq": seq_at(3, 0)}, {"seq": seq_at(0, 1)}
    here = lax.axis_index("seq")
    half = parts.shape[1] // 2
    top, bottom = pl.ds(0, half), pl.ds(half, half)
    state = {}

    def first(make):
        make(seq_at(2, 1))
        state["c1"] = wires.send(parts.at[seq_at(2, 1)], inbox.at[0], up)
        make(seq_at(3, 1))
        state["c2"] = wires.send(parts.at[seq_at(3, 1)], inbox.at[1], down)
        far = seq_at(2, 0)
        make(far)
        state["ct"] = wires.send(parts.at[far, top], inbox.at[2, top], down)
        state["cb"] = wires.send(parts.at[far, bottom], inbox.at[2, bottom], up)

    def second():
        state["c1"].wait_recv()
        inbox[0] = inbox[0] + parts[seq_at(1, 1)]
        state["c4"] = wires.send(inbox.at[0], inbox.at[3], across)
        state["c2"].wait_recv()
        inbox[1] = inbox[1] + parts[seq_at(0, 1)]
        state["c5"] = wires.send(inbox.at[1], inbox.at[4], across)
        to = seq_at(3, 0)
        state["c6b"] = wires.send(parts.at[to, bottom], inbox.at[5, bottom], down)
        state["ct"].wait_recv()
        inbox[2, top] = inbox[2, top] + parts[to, top]
        state["c6t"] = wires.send(inbox.at[2, top], inbox.at[5, top], down)

    def third():
        state["cb"].wait_recv()
        state["c4"].wait_recv()
        to = seq_at(1, 0)
        inbox[3] = (parts[to].astype(F32) + inbox[3].astype(F32)).astype(BF16)
        inbox[3, bottom] = inbox[3, bottom] + inbox[2, bottom]
        state["c7"] = wires.send(inbox.at[3], inbox.at[6], up)

    def last():
        for name in ("c5", "c6b", "c6t", "c7"):
            state[name].wait_recv()
        return (parts[here].astype(F32) + inbox[4].astype(F32)) + (
            inbox[5].astype(F32) + inbox[6].astype(F32)
        )

    return first, second, third, last


SCATTER_SENDS = 9


def total_steps(wires, terms, acc, above, below, beside, out):
    core = lax.rem(lax.axis_index("dp"), 2)
    z = lax.rem(lax.axis_index("dp") // 2, 8)
    xh = lax.axis_index("dp") // 16
    twin, up, down = {"dp": dp_at(0, 0, 1)}, {"dp": dp_at(0, 1, 0)}, {"dp": dp_at(0, 7, 0)}
    far = {"dp": dp_at(1, 0, 0)}
    state = {}

    def at(dz):
        return lax.rem(z + dz, 8)

    def start():
        state["twin"] = wires.send(terms.at[:, 1 - core], acc, twin)

    def first():
        state["twin"].wait_recv()
        chips = terms.shape[0]

        @pl.loop(0, chips)
        def _(chip):
            acc[chip] = acc[chip] + terms[chip, core]

        state["u"] = wires.send(acc.at[at(4)], above.at[0, 0], up)
        state["d"] = wires.send(acc.at[8 + at(4)], below.at[0, 1], down)

    def middle(step):
        def run():
            to_up, to_down = at(4 - step), at(4 + step)
            state["u"].wait_recv()
            acc[to_up] = acc[to_up] + above[step - 1, 0]
            if step > 1:
                acc[8 + to_up] = acc[8 + to_up] + above[step - 1, 1]
            state["u0"] = wires.send(acc.at[to_up], above.at[step, 0], up)
            state["u1"] = wires.send(acc.at[8 + to_up], above.at[step, 1], up)
            state["d"].wait_recv()
            acc[8 + to_down] = acc[8 + to_down] + below[step - 1, 1]
            if step > 1:
                acc[to_down] = acc[to_down] + below[step - 1, 0]
            state["d0"] = wires.send(acc.at[to_down], below.at[step, 0], down)
            state["d1"] = wires.send(acc.at[8 + to_down], below.at[step, 1], down)
            state["u"], state["d"] = Both(state["u0"], state["u1"]), Both(state["d0"], state["d1"])

        return run

    def cross():
        state["u"].wait_recv()
        state["d"].wait_recv()
        other = 1 - xh
        to = other * 8 + z
        acc[to] = (
            acc[to].astype(F32) + above[3, other].astype(F32) + below[3, other].astype(F32)
        ).astype(BF16)
        state["far"] = wires.send(acc.at[to], beside, far)

    def last():
        state["far"].wait_recv()
        total = acc[xh * 8 + z].astype(F32) + above[3, xh].astype(F32)
        out[...] = (total + below[3, xh].astype(F32) + beside[...].astype(F32)).astype(BF16)

    return start, first, middle(1), middle(2), middle(3), cross, last


TOTAL_SENDS = 1 + 2 + 3 * 4 + 1


class Both:
    def __init__(self, *copies):
        self.copies = copies

    def wait_recv(self):
        for copy in self.copies:
            copy.wait_recv()


def total_scratch(rows, columns):
    return [
        VMEM((16, rows, columns), BF16),
        VMEM((4, 2, rows, columns), BF16),
        VMEM((4, 2, rows, columns), BF16),
        VMEM((rows, columns), BF16),
    ]


def sems(count):
    return [pltpu.SemaphoreType.DMA((count,)), pltpu.SemaphoreType.DMA((count,))]


def weight_steps(wires, block, blocks):
    core = lax.rem(lax.axis_index("dp"), 2)
    z = lax.rem(lax.axis_index("dp") // 2, 8)
    xh = lax.axis_index("dp") // 16
    twin, up, down = {"dp": dp_at(0, 0, 1)}, {"dp": dp_at(0, 1, 0)}, {"dp": dp_at(0, 7, 0)}
    far = {"dp": dp_at(1, 0, 0)}
    state = {}

    def at(dz):
        return lax.rem(z + dz, 8)

    def start():
        state["far"] = wires.send(block, blocks.at[z, xh, core], far)

    def pass_on(step):
        def run():
            if step == 0:
                state["far"].wait_recv()
            else:
                state["up"].wait_recv()
                state["down"].wait_recv()
            low, high = at(8 - step), at(step)
            if step < 3:
                above, below = blocks.at[low, :, core], blocks.at[high, :, core]
            else:
                above, below = blocks.at[low, 0, core], blocks.at[high, 1, core]
            state["up"] = wires.send(above, above, up)
            state["down"] = wires.send(below, below, down)

        return run

    def share():
        state["up"].wait_recv()
        state["down"].wait_recv()
        part = blocks.at[:, :, core]
        state["twin"] = wires.send(part, part, twin)

    def last():
        state["twin"].wait_recv()

    return start, pass_on(0), pass_on(1), pass_on(2), pass_on(3), share, last


WEIGHT_SENDS = 1 + 8 + 1


def iotas(shape):
    return lax.broadcasted_iota(jnp.int32, shape, 0), lax.broadcasted_iota(jnp.int32, shape, 1)


def one_hot(slot, column, group, slots, offset):
    shift = slots.bit_length() - 1
    device, inside = lax.shift_right_logical(slot, shift), lax.bitwise_and(slot, slots - 1)
    within = jnp.logical_and(inside >= offset, inside < offset + group)
    hit = jnp.logical_and(device * group + inside - offset == column, within)
    return jnp.where(hit, 1.0, 0.0).astype(BF16)


def ring_slot(slot):
    z = lax.shift_right_logical(slot, 7)
    xh = lax.bitwise_and(lax.shift_right_logical(slot, 6), 1)
    return xh * 512 + z * 64 + lax.bitwise_and(slot, 63)


def dot(a, b, dims):
    return lax.dot_general(a, b, (dims, ((), ())), preferred_element_type=F32)


NN, NT, TN = ((1,), (0,)), ((1,), (1,)), ((0,), (0,))


def kernel(
    inputs, saved, attn, upstream, w_qkv, w_out, w_block,
    grad_rows, qkv_sum, out_sum, conv_sum_a, conv_sum_b,
    saved_all, upstream_all, mid_pad, gelu_pad, attn_all, gelu_out_blocks, attn_blocks, slope,
    blocks, normed, proj, expo, sums, grad_attn, query_acc, grad_proj, parts, inbox,
    qkv_terms, out_terms, gelu_wide, w_taps, conv_a, conv_b, gelu_send, gelu_back,
    q0, q1, q2, q3, o0, o1, o2, o3, a0, a1, a2, a3, b0, b1, b2, b3,
    send_sems, recv_sems, own_sems,
):
    here = lax.axis_index("seq")
    core = lax.rem(lax.axis_index("dp"), 2)
    z = lax.rem(lax.axis_index("dp") // 2, 8)
    xh = lax.axis_index("dp") // 16
    rows, channels = saved.shape
    length = 8 * rows
    width = w_out.shape[0]
    half = channels // 2
    scale = HD ** (-0.5)
    meet(
        [{"seq": seq_at(*offset)} for offset in SEQ_OFFSETS]
        + [{"dp": dp_at(*offset)} for offset in ((0, 0, 1), (0, 1, 0), (0, 7, 0), (1, 0, 0))]
    )
    wires = Wires(send_sems, recv_sems)

    def span(s, start=0, count=rows, base=0):
        return pl.ds(pl.multiple_of(s * rows + (base + start), 32), count)

    def place_of(ref, base=0):
        return lambda s, start, count: ref.at[span(s, start, count, base)]

    get_saved = gather_steps(wires, saved, place_of(saved_all), rows)
    get_upstream = gather_steps(wires, upstream, place_of(upstream_all), rows)
    get_weight = weight_steps(wires, w_block, blocks)
    get_saved[0]()
    get_weight[0]()
    kept = [
        pltpu.make_async_copy(saved, saved_all.at[span(here)], own_sems.at[0]),
        pltpu.make_async_copy(upstream, upstream_all.at[span(here)], own_sems.at[1]),
        pltpu.make_async_copy(w_block, blocks.at[z, xh, core], own_sems.at[2]),
    ]
    for copy in kept:
        copy.start()

    pair = 2 * width
    row_of, column_of = iotas((pair, width))
    picks = [(row_of == column_of + part * width) for part in range(2)]
    picks = [jnp.where(pick, 1.0, 0.0).astype(BF16) for pick in picks]
    for index in range(4):
        columns = pl.ds(index * pair, pair)
        value = inputs[:, columns].astype(F32)
        cubic = value * value * 0.044715
        inner = math.sqrt(2.0 / math.pi) * value * (1.0 + cubic)
        bend = jnp.tanh(inner)
        gelu = (0.5 * value * (1.0 + bend)).astype(BF16)
        slope[:, columns] = 0.5 * (1.0 + bend) + 0.5 * value * (1.0 - bend * bend) * (
            math.sqrt(2.0 / math.pi) * (1.0 + 3.0 * cubic)
        )
        attn_pair = attn[:, columns]
        for part in range(2):
            gelu_out_blocks[2 * index + part] = dot(gelu, picks[part], NN).astype(BF16)
            attn_blocks[2 * index + part] = dot(attn_pair, picks[part], NN).astype(BF16)
    zeros = jnp.zeros((REACH, channels), BF16)
    mid_pad[pl.ds(0, REACH)] = zeros
    mid_pad[pl.ds(REACH + length, REACH)] = zeros
    gelu_pad[pl.ds(0, REACH)] = zeros[:, :width]
    gelu_pad[pl.ds(REACH + length, REACH)] = zeros[:, :width]
    for copy in kept:
        copy.wait()

    def project(s):
        at = span(s)
        wide = saved_all[at].astype(F32)
        inverse = lax.rsqrt(jnp.mean(wide * wide, axis=-1, keepdims=True) + EPSILON)
        block = (wide * inverse).astype(BF16)
        normed[at] = block
        for j in range(3):
            proj[j, at] = dot(block, w_qkv[j], NT).astype(BF16)

    def project_all(offsets):
        for offset in offsets:
            project(seq_at(*offset))

    project_all([(0, 0)])
    get_saved[1]()
    get_upstream[0]()
    get_weight[1]()
    project_all([(3, 0), (1, 0), (0, 1)])
    get_saved[2]()
    get_weight[2]()
    project_all([(1, 1)])
    get_saved[3]()
    get_weight[3]()
    project_all([(2, 0), (3, 1), (2, 1)])
    get_upstream[1]()
    swapped = []
    for offset in SEQ_OFFSETS:
        to = seq_at(*offset)
        swapped.append(wires.send(attn_blocks.at[to], attn_all.at[span(here)], {"seq": to}))
        swapped.append(
            wires.send(gelu_out_blocks.at[to], gelu_pad.at[span(here, base=REACH)], {"seq": to})
        )
    attn_all[span(here)] = attn_blocks[here]
    gelu_pad[span(here, base=REACH)] = gelu_out_blocks[here]
    get_weight[4]()

    tile = 256
    sums[...] = jnp.zeros_like(sums)

    @pl.loop(0, length // tile)
    def _(index):
        at = pl.ds(pl.multiple_of(index * tile, tile), tile)
        weight = jnp.exp(dot(proj[1, at], proj[0], NT) * scale)
        expo[at] = weight
        sums[...] += jnp.sum(weight, axis=0, keepdims=True)

    def attend(s):
        at = span(s)
        grad_attn[at] = dot(upstream_all[at], w_out[...], NT).astype(BF16)

    def attend_all(offsets):
        for offset in offsets:
            attend(seq_at(*offset))

    attend_all([(0, 0), (3, 0), (1, 0), (0, 1)])
    get_upstream[2]()
    get_weight[5]()
    attend_all([(1, 1)])
    get_upstream[3]()
    attend_all([(2, 0), (3, 1), (2, 1)])
    for copy in swapped:
        copy.wait_recv()

    product = grad_attn[...].astype(F32) * attn_all[...].astype(F32)
    delta = lax.dot_general(
        jnp.ones((8, width), F32), product, (NT, ((), ())),
        precision=lax.Precision.HIGHEST, preferred_element_type=F32,
    )[0:1]
    ratio = 1.0 / sums[...]
    query_acc[...] = jnp.zeros_like(query_acc)

    @pl.loop(0, length // tile)
    def _(index):
        at = pl.ds(pl.multiple_of(index * tile, tile), tile)
        probs = expo[at] * ratio
        grad_prob = dot(proj[2, at], grad_attn[...], NT)
        score = (probs * (grad_prob - delta) * scale).astype(BF16)
        grad_proj[1, at] = dot(score, proj[0], NN).astype(BF16)
        grad_proj[2, at] = dot(probs.astype(BF16), grad_attn[...], NN).astype(BF16)
        query_acc[...] += dot(score, proj[1, at], TN)

    grad_proj[0] = query_acc[...].astype(BF16)

    def acts(s):
        at = span(s)

        @pl.loop(0, channels // 512)
        def _(index):
            columns = pl.ds(pl.multiple_of(index * 512, 512), 512)
            total = dot(grad_proj[0, at], w_qkv[0, :, columns], NN)
            total += dot(grad_proj[1, at], w_qkv[1, :, columns], NN)
            total += dot(grad_proj[2, at], w_qkv[2, :, columns], NN)
            parts[s, :, columns] = total.astype(BF16)

    scatter = scatter_steps(wires, parts, inbox)
    scatter[0](acts)
    for offset in ((1, 1), (0, 1), (3, 0), (1, 0), (0, 0)):
        acts(seq_at(*offset))

    sum_qkv = total_steps(wires, qkv_terms, q0, q1, q2, q3, qkv_sum)
    sum_out = total_steps(wires, out_terms, o0, o1, o2, o3, out_sum)

    @pl.loop(0, 4)
    def _(index):
        columns = pl.ds(pl.multiple_of(index * 384, 384), 384)
        turned = normed[:, columns].T
        for j in range(3):
            result = dot(turned, grad_proj[j], NN).astype(BF16)
            qkv_terms[pl.ds(index * 4, 4), :, pl.ds(j * 48, 48)] = result.reshape(4, 2, 48, width)

    sum_qkv[0]()
    scatter[1]()
    slot_of, column_of = iotas((512, width))
    for part in range(2):
        pick = one_hot(slot_of, column_of, 6, 16, 6 * part)
        gelu_wide[pl.ds(512 * part, 512)] = dot(pick, attn_all[...], NT).astype(BF16)

    @pl.loop(0, 3)
    def _(index):
        first = dot(gelu_wide[pl.ds(0, 512)], upstream_all[:, pl.ds(pl.multiple_of(index * 256, 256), 256)], NN)
        second = dot(
            gelu_wide[pl.ds(512, 512)], upstream_all[:, pl.ds(pl.multiple_of(half + index * 256, 256), 256)], NN
        )
        result = (first + second).astype(BF16).reshape(16, 2, 16, 256)
        out_terms[:, :, :, pl.ds(pl.multiple_of(index * 256, 256), 256)] = result

    sum_out[0]()
    sum_qkv[1]()
    scatter[2]()
    sum_out[1]()

    slot_of, column_of = iotas((tile, width))

    @pl.loop(0, 4)
    def _(index):
        total = jnp.zeros((tile, length), F32)
        for tap in range(TAPS):
            pick = one_hot(slot_of + index * tile, column_of, 6, 32, 6 * tap)
            total += dot(pick, gelu_pad[pl.ds(DILATION * tap, length)], NT)
        gelu_wide[pl.ds(pl.multiple_of(index * tile, tile), tile)] = total.astype(BF16)

    sum_qkv[2]()
    sum_out[2]()
    acts_here = scatter[3]()
    wide = saved[...].astype(F32)
    inverse = lax.rsqrt(jnp.mean(wide * wide, axis=-1, keepdims=True) + EPSILON)
    straight = wide * inverse
    grad = inverse * (
        acts_here - straight * jnp.mean(acts_here * straight, axis=-1, keepdims=True)
    )
    at_mine = span(here, base=REACH)
    mid_pad[at_mine] = (upstream[...].astype(F32) + grad).astype(BF16)
    get_mid = gather_steps(wires, mid_pad.at[at_mine], place_of(mid_pad, REACH), rows)
    get_mid[0]()
    sum_qkv[3]()
    sum_out[3]()

    get_weight[6]()
    row_of, slot_of = iotas((width, length))

    for tap in range(TAPS):
        pick = one_hot(ring_slot(slot_of), row_of, 6, 32, 6 * tap)

        @pl.loop(0, 3)
        def _(index):
            columns = pl.ds(pl.multiple_of(index * 512, 512), 512)
            weight = blocks[:, :, :, :, columns].reshape(length, 512)
            w_taps[tap, :, columns] = dot(pick, weight, NN).astype(BF16)

    get_mid[1]()
    sum_qkv[4]()
    sum_out[4]()
    get_mid[2]()
    sum_qkv[5]()
    sum_out[5]()
    sum_qkv[6]()
    sum_out[6]()
    get_mid[3]()

    totals = [
        total_steps(wires, conv_a, a0, a1, a2, a3, conv_sum_a),
        total_steps(wires, conv_b, b0, b1, b2, b3, conv_sum_b),
    ]
    for part, terms in enumerate((conv_a, conv_b)):

        @pl.loop(0, 4)
        def _(index):
            at = pl.ds(pl.multiple_of(index * tile, tile), tile)
            for column in range(0, half, 256):
                result = dot(
                    gelu_wide[at],
                    mid_pad[pl.ds(REACH, length), pl.ds(part * half + column, 256)],
                    NN,
                ).astype(BF16)
                terms[pl.ds(index * 4, 4), :, :, pl.ds(column, 256)] = result.reshape(4, 2, 32, 256)

        totals[part][0]()

    @pl.loop(0, length // tile)
    def _(index):
        total = jnp.zeros((tile, width), F32)
        for tap in range(TAPS):
            at = pl.ds(pl.multiple_of(index * tile + (2 * REACH - DILATION * tap), 32), tile)
            total += dot(mid_pad[at], w_taps[tap], NT)
        gelu_send[pl.ds(index * 2, 2)] = total.astype(BF16).reshape(2, rows, width)

    for steps in totals:
        steps[1]()
    swapped = []
    for offset in SEQ_OFFSETS:
        to = seq_at(*offset)
        swapped.append(wires.send(gelu_send.at[to], gelu_back.at[here], {"seq": to}))
    gelu_back[here] = gelu_send[here]
    for step in range(2, 5):
        for steps in totals:
            steps[step]()
    for copy in swapped:
        copy.wait_recv()
    for index in range(4):
        columns = pl.ds(index * pair, pair)
        gelu_grad = dot(gelu_back[2 * index], picks[0], NT) + dot(
            gelu_back[2 * index + 1], picks[1], NT
        )
        grad_rows[:, columns] = (
            mid_pad[at_mine, columns].astype(F32) + slope[:, columns] * gelu_grad
        ).astype(BF16)
    for step in range(5, 7):
        for steps in totals:
            steps[step]()
    wires.finish()


def run(inputs, saved, attn, upstream, w_qkv, w_out, w_block):
    rows, channels = saved.shape
    length, width, half = 8 * rows, w_out.shape[0], channels // 2
    count = 3 * GATHER_SENDS + SCATTER_SENDS + WEIGHT_SENDS + 3 * 7 + 4 * TOTAL_SENDS
    in_vmem = pl.BlockSpec(memory_space=VMEM)
    return pl.pallas_call(
        kernel,
        out_shape=[
            jax.ShapeDtypeStruct((rows, channels), BF16),
            jax.ShapeDtypeStruct((144, width), BF16),
            jax.ShapeDtypeStruct((16, half), BF16),
            jax.ShapeDtypeStruct((32, half), BF16),
            jax.ShapeDtypeStruct((32, half), BF16),
        ],
        in_specs=[in_vmem] * 7,
        out_specs=[in_vmem] * 5,
        scratch_shapes=[
            VMEM((length, channels), BF16),
            VMEM((length, channels), BF16),
            VMEM((length + 2 * REACH, channels), BF16),
            VMEM((length + 2 * REACH, width), BF16),
            VMEM((length, width), BF16),
            VMEM((8, rows, width), BF16),
            VMEM((8, rows, width), BF16),
            VMEM((rows, channels), F32),
            VMEM((8, 2, 2, 32, channels), BF16),
            VMEM((length, channels), BF16),
            VMEM((3, length, width), BF16),
            VMEM((length, length), F32),
            VMEM((1, length), F32),
            VMEM((length, width), BF16),
            VMEM((length, width), F32),
            VMEM((3, length, width), BF16),
            VMEM((8, rows, channels), BF16),
            VMEM((7, rows, channels), BF16),
            VMEM((16, 2, 144, width), BF16),
            VMEM((16, 2, 16, half), BF16),
            VMEM((length, length), BF16),
            VMEM((TAPS, width, channels), BF16),
            VMEM((16, 2, 32, half), BF16),
            VMEM((16, 2, 32, half), BF16),
            VMEM((8, rows, width), BF16),
            VMEM((8, rows, width), BF16),
        ]
        + total_scratch(144, width)
        + total_scratch(16, half)
        + total_scratch(32, half)
        + total_scratch(32, half)
        + sems(count)
        + [pltpu.SemaphoreType.DMA((3,))],
        compiler_params=pltpu.CompilerParams(
            collective_id=1, has_side_effects=True, vmem_limit_bytes=58 << 20
        ),
    )(inputs, saved, attn, upstream, w_qkv, w_out, w_block)


def local(inputs, saved, attn_saved, upstream, w_qkv, w_out, w_conv):
    channels = inputs.shape[2]
    width = w_out.shape[0]
    taps_rows = w_conv.shape[0] * w_conv.shape[1]
    w_block = jnp.pad(w_conv.reshape(taps_rows, channels), ((0, 32 - taps_rows), (0, 0)))
    grad_rows, qkv_sum, out_sum, sum_a, sum_b = run(
        inputs[0], saved[0], attn_saved[0], upstream[0], w_qkv.transpose(1, 2, 0), w_out, w_block
    )
    out_pair = out_sum[:12].reshape(2, 6, channels // 2)
    return (
        grad_rows[None],
        qkv_sum.reshape(3, channels // 32, width).transpose(1, 0, 2),
        jnp.concatenate([out_pair[0], out_pair[1]], axis=1),
        jnp.concatenate([sum_a, sum_b], axis=1)[:taps_rows].reshape(w_conv.shape),
    )


def solution(mesh):
    placed = (
        P("dp", "seq", None),
        P("dp", "seq", None),
        P("dp", "seq", None),
        P("dp", "seq", None),
        P(None, None, "seq"),
        P("seq", None),
        P(None, ("seq", "dp"), None),
    )
    return jax.shard_map(
        local,
        mesh=mesh,
        in_specs=placed,
        out_specs=(
            P("dp", "seq", None),
            P("dp", None, "seq"),
            P(("seq", "dp"), None),
            P(None, ("seq", "dp"), None),
        ),
        check_vma=False,
    )
```

```python
import math

import jax
import jax.numpy as jnp
from jax import lax
from jax.experimental import pallas as pl
from jax.experimental.pallas import tpu as pltpu
from jax.sharding import PartitionSpec as P

HD = 192
TAPS = 5
DILATION = 32
EPSILON = 1e-06
REACH = DILATION * (TAPS // 2)
BF16 = jnp.bfloat16
F32 = jnp.float32
MESH = pl.DeviceIdType.MESH
VMEM = pltpu.VMEM
ANY = pl.ANY


def seq_at(dy, dx):
    here = lax.axis_index("seq")
    return lax.rem(here // 2 + dy, 4) * 2 + lax.rem(here + dx, 2)


def dp_at(dxh, dz, dcore):
    here = lax.axis_index("dp")
    core = lax.rem(here + dcore, 2)
    z = lax.rem(here // 2 + dz, 8)
    xh = lax.rem(here // 16 + dxh, 2)
    return (xh * 8 + z) * 2 + core


SEQ_OFFSETS = [(dy, dx) for dy in (2, 1, 3, 0) for dx in (1, 0) if (dy, dx) != (0, 0)]


def meet(peers):
    barrier = pltpu.get_barrier_semaphore()
    for peer in peers:
        pl.semaphore_signal(barrier, inc=1, device_id=peer, device_id_type=MESH)
    pl.semaphore_wait(barrier, len(peers))


class Wires:
    def __init__(self, send_sems, recv_sems):
        self.send_sems, self.recv_sems = send_sems, recv_sems
        self.used = 0
        self.copies = []

    def send(self, source, target, device):
        copy = pltpu.make_async_remote_copy(
            source,
            target,
            self.send_sems.at[self.used],
            self.recv_sems.at[self.used],
            device_id=device,
            device_id_type=MESH,
        )
        copy.start()
        self.used += 1
        self.copies.append(copy)
        return copy

    def finish(self):
        for copy in self.copies:
            copy.wait_send()


def gather_steps(wires, source, whole, base, rows):
    def place(s, start, count):
        return whole(s, base + start, count)

    up, down, across = {"seq": seq_at(1, 0)}, {"seq": seq_at(3, 0)}, {"seq": seq_at(0, 1)}
    half = rows // 2
    state = {}

    def first():
        mine = place(lax.axis_index("seq"), 0, rows)
        state["up"] = wires.send(source, mine, up)
        state["down"] = wires.send(source, mine, down)
        state["across"] = wires.send(source, mine, across)

    def second():
        state["up"].wait_recv()
        part = place(seq_at(3, 0), 0, half)
        state["far_up"] = wires.send(part, part, up)
        state["down"].wait_recv()
        part = place(seq_at(1, 0), half, half)
        state["far_down"] = wires.send(part, part, down)
        part = place(seq_at(1, 0), 0, rows)
        state["over"] = wires.send(part, part, across)
        state["across"].wait_recv()
        part = place(seq_at(0, 1), 0, rows)
        state["side_up"] = wires.send(part, part, up)

    def third():
        state["over"].wait_recv()
        part = place(seq_at(1, 1), 0, rows)
        state["side_down"] = wires.send(part, part, down)

    def last():
        for name in ("far_up", "far_down", "side_up", "side_down"):
            state[name].wait_recv()

    return first, second, third, last


GATHER_SENDS = 8


def scatter_steps(wires, parts, inbox, base, rows):
    up, down, across = {"seq": seq_at(1, 0)}, {"seq": seq_at(3, 0)}, {"seq": seq_at(0, 1)}
    here = lax.axis_index("seq")
    every = pl.ds(base, rows)
    top, bottom = pl.ds(base, rows // 2), pl.ds(base + rows // 2, rows // 2)
    state = {}

    def post(name, source, target, device):
        state[name] = wires.send(source, target, device)

    def far_side_up():
        post("c1", parts.at[seq_at(2, 1), every], inbox.at[0, every], up)

    def far_side_down():
        post("c2", parts.at[seq_at(3, 1), every], inbox.at[1, every], down)

    def far():
        post("ct", parts.at[seq_at(2, 0), top], inbox.at[2, top], down)
        post("cb", parts.at[seq_at(2, 0), bottom], inbox.at[2, bottom], up)

    def across_first():
        state["c1"].wait_recv()
        inbox[0, every] = inbox[0, every] + parts[seq_at(1, 1), every]
        post("c4", inbox.at[0, every], inbox.at[3, every], across)

    def across_second():
        state["c2"].wait_recv()
        inbox[1, every] = inbox[1, every] + parts[seq_at(0, 1), every]
        post("c5", inbox.at[1, every], inbox.at[4, every], across)

    def near_down():
        to = seq_at(3, 0)
        post("c6b", parts.at[to, bottom], inbox.at[5, bottom], down)
        state["ct"].wait_recv()
        inbox[2, top] = inbox[2, top] + parts[to, top]
        post("c6t", inbox.at[2, top], inbox.at[5, top], down)

    def near_up():
        state["cb"].wait_recv()
        state["c4"].wait_recv()
        to = seq_at(1, 0)
        inbox[3, every] = (parts[to, every].astype(F32) + inbox[3, every].astype(F32)).astype(BF16)
        inbox[3, bottom] = inbox[3, bottom] + inbox[2, bottom]
        post("c7", inbox.at[3, every], inbox.at[6, every], up)

    def last():
        for name in ("c5", "c6b", "c6t", "c7"):
            state[name].wait_recv()
        return (parts[here, every].astype(F32) + inbox[4, every].astype(F32)) + (
            inbox[5, every].astype(F32) + inbox[6, every].astype(F32)
        )

    return far_side_up, far_side_down, far, across_first, across_second, near_down, near_up, last


SCATTER_SENDS = 9


def total_steps(wires, terms, acc, above, below, beside, out):
    core = lax.rem(lax.axis_index("dp"), 2)
    z = lax.rem(lax.axis_index("dp") // 2, 8)
    xh = lax.axis_index("dp") // 16
    twin, up, down = {"dp": dp_at(0, 0, 1)}, {"dp": dp_at(0, 1, 0)}, {"dp": dp_at(0, 7, 0)}
    far = {"dp": dp_at(1, 0, 0)}
    state = {}

    def at(dz):
        return lax.rem(z + dz, 8)

    def start():
        state["twin"] = wires.send(terms.at[:, 1 - core], acc, twin)

    def first():
        state["twin"].wait_recv()
        chips = terms.shape[0]

        @pl.loop(0, chips)
        def _(chip):
            acc[chip] = acc[chip] + terms[chip, core]

        state["u"] = wires.send(acc.at[at(4)], above.at[0, 0], up)
        state["d"] = wires.send(acc.at[8 + at(4)], below.at[0, 1], down)

    def middle(step):
        def run():
            to_up, to_down = at(4 - step), at(4 + step)
            state["u"].wait_recv()
            acc[to_up] = acc[to_up] + above[step - 1, 0]
            if step > 1:
                acc[8 + to_up] = acc[8 + to_up] + above[step - 1, 1]
            state["u0"] = wires.send(acc.at[to_up], above.at[step, 0], up)
            state["u1"] = wires.send(acc.at[8 + to_up], above.at[step, 1], up)
            state["d"].wait_recv()
            acc[8 + to_down] = acc[8 + to_down] + below[step - 1, 1]
            if step > 1:
                acc[to_down] = acc[to_down] + below[step - 1, 0]
            state["d0"] = wires.send(acc.at[to_down], below.at[step, 0], down)
            state["d1"] = wires.send(acc.at[8 + to_down], below.at[step, 1], down)
            state["u"], state["d"] = Both(state["u0"], state["u1"]), Both(state["d0"], state["d1"])

        return run

    def cross():
        state["u"].wait_recv()
        state["d"].wait_recv()
        other = 1 - xh
        to = other * 8 + z
        acc[to] = (
            acc[to].astype(F32) + above[3, other].astype(F32) + below[3, other].astype(F32)
        ).astype(BF16)
        state["far"] = wires.send(acc.at[to], beside, far)

    def last():
        state["far"].wait_recv()
        total = acc[xh * 8 + z].astype(F32) + above[3, xh].astype(F32)
        out[...] = (total + below[3, xh].astype(F32) + beside[...].astype(F32)).astype(BF16)

    return start, first, middle(1), middle(2), middle(3), cross, last


TOTAL_SENDS = 1 + 2 + 3 * 4 + 1


class Both:
    def __init__(self, *copies):
        self.copies = copies

    def wait_recv(self):
        for copy in self.copies:
            copy.wait_recv()


def total_scratch(rows, columns):
    return [
        VMEM((16, rows, columns), BF16),
        VMEM((4, 2, rows, columns), BF16),
        VMEM((4, 2, rows, columns), BF16),
        VMEM((rows, columns), BF16),
    ]


def sems(count):
    return [pltpu.SemaphoreType.DMA((count,)), pltpu.SemaphoreType.DMA((count,))]


def weight_steps(wires, block, blocks):
    core = lax.rem(lax.axis_index("dp"), 2)
    z = lax.rem(lax.axis_index("dp") // 2, 8)
    xh = lax.axis_index("dp") // 16
    twin, up, down = {"dp": dp_at(0, 0, 1)}, {"dp": dp_at(0, 1, 0)}, {"dp": dp_at(0, 7, 0)}
    far = {"dp": dp_at(1, 0, 0)}
    state = {}

    def at(dz):
        return lax.rem(z + dz, 8)

    def start():
        state["far"] = wires.send(block, blocks.at[z, xh, core], far)

    def pass_on(step):
        def run():
            if step == 0:
                state["far"].wait_recv()
            else:
                state["up"].wait_recv()
                state["down"].wait_recv()
            low, high = at(8 - step), at(step)
            if step < 3:
                above, below = blocks.at[low, :, core], blocks.at[high, :, core]
            else:
                above, below = blocks.at[low, 0, core], blocks.at[high, 1, core]
            state["up"] = wires.send(above, above, up)
            state["down"] = wires.send(below, below, down)

        return run

    def share():
        state["up"].wait_recv()
        state["down"].wait_recv()
        part = blocks.at[:, :, core]
        state["twin"] = wires.send(part, part, twin)

    def last():
        state["twin"].wait_recv()

    return start, pass_on(0), pass_on(1), pass_on(2), pass_on(3), share, last


WEIGHT_SENDS = 1 + 8 + 1


def iotas(shape):
    return lax.broadcasted_iota(jnp.int32, shape, 0), lax.broadcasted_iota(jnp.int32, shape, 1)


def one_hot(slot, column, group, slots, offset):
    shift = slots.bit_length() - 1
    device, inside = lax.shift_right_logical(slot, shift), lax.bitwise_and(slot, slots - 1)
    within = jnp.logical_and(inside >= offset, inside < offset + group)
    hit = jnp.logical_and(device * group + inside - offset == column, within)
    return jnp.where(hit, 1.0, 0.0).astype(BF16)


def ring_slot(slot):
    z = lax.shift_right_logical(slot, 7)
    xh = lax.bitwise_and(lax.shift_right_logical(slot, 6), 1)
    return xh * 512 + z * 64 + lax.bitwise_and(slot, 63)


def dot(a, b, dims):
    return lax.dot_general(a, b, (dims, ((), ())), preferred_element_type=F32)


NN, NT, TN = ((1,), (0,)), ((1,), (1,)), ((0,), (0,))


def kernel(
    inputs, saved, attn, upstream, w_qkv, w_out, w_block,
    grad_rows, qkv_sum, out_sum, conv_sum_a, conv_sum_b,
    saved_all, upstream_all, mid_pad, gelu_pad, attn_all, gelu_out_blocks, attn_blocks, slope,
    blocks, normed, proj, expo, sums, grad_attn, query_acc, grad_proj, parts, inbox,
    qkv_terms, out_terms, gelu_wide, w_taps, conv_a, conv_b, gelu_send, gelu_back,
    q0, q1, q2, q3, o0, o1, o2, o3, a0, a1, a2, a3, b0, b1, b2, b3,
    send_sems, recv_sems, own_sems,
):
    here = lax.axis_index("seq")
    core = lax.rem(lax.axis_index("dp"), 2)
    z = lax.rem(lax.axis_index("dp") // 2, 8)
    xh = lax.axis_index("dp") // 16
    rows, channels = saved.shape
    length = 8 * rows
    width = w_out.shape[0]
    half = channels // 2
    scale = HD ** (-0.5)
    meet(
        [{"seq": seq_at(*offset)} for offset in SEQ_OFFSETS]
        + [{"dp": dp_at(*offset)} for offset in ((0, 0, 1), (0, 1, 0), (0, 7, 0), (1, 0, 0))]
    )
    wires = Wires(send_sems, recv_sems)

    def span(s, start=0, count=rows, base=0):
        return pl.ds(pl.multiple_of(s * rows + (base + start), 32), count)

    def place_of(ref, base=0):
        return lambda s, start, count: ref.at[span(s, start, count, base)]

    half_rows = rows // 2

    def halves(source, whole):
        return [
            gather_steps(wires, source(part * half_rows), whole, part * half_rows, half_rows)
            for part in range(2)
        ]

    def rows_of(ref):
        return lambda start: ref.at[pl.ds(start, half_rows)]

    get_saved = halves(rows_of(saved), place_of(saved_all))
    get_upstream = halves(rows_of(upstream), place_of(upstream_all))
    get_mid = halves(lambda start: mid_pad.at[span(here, start, half_rows, REACH)], place_of(mid_pad, REACH))
    get_weight = weight_steps(wires, w_block, blocks)
    get_saved[0][0]()
    get_saved[1][0]()
    get_weight[0]()
    kept = [
        pltpu.make_async_copy(saved, saved_all.at[span(here)], own_sems.at[0]),
        pltpu.make_async_copy(upstream, upstream_all.at[span(here)], own_sems.at[1]),
        pltpu.make_async_copy(w_block, blocks.at[z, xh, core], own_sems.at[2]),
    ]
    for copy in kept:
        copy.start()

    pair = 2 * width
    row_of, column_of = iotas((pair, width))
    picks = [(row_of == column_of + part * width) for part in range(2)]
    picks = [jnp.where(pick, 1.0, 0.0).astype(BF16) for pick in picks]
    for index in range(4):
        columns = pl.ds(index * pair, pair)
        value = inputs[:, columns].astype(F32)
        cubic = value * value * 0.044715
        inner = math.sqrt(2.0 / math.pi) * value * (1.0 + cubic)
        bend = jnp.tanh(inner)
        gelu = (0.5 * value * (1.0 + bend)).astype(BF16)
        slope[:, columns] = 0.5 * (1.0 + bend) + 0.5 * value * (1.0 - bend * bend) * (
            math.sqrt(2.0 / math.pi) * (1.0 + 3.0 * cubic)
        )
        attn_pair = attn[:, columns]
        for part in range(2):
            gelu_out_blocks[2 * index + part] = dot(gelu, picks[part], NN).astype(BF16)
            attn_blocks[2 * index + part] = dot(attn_pair, picks[part], NN).astype(BF16)
    zeros = jnp.zeros((REACH, channels), BF16)
    mid_pad[pl.ds(0, REACH)] = zeros
    mid_pad[pl.ds(REACH + length, REACH)] = zeros
    gelu_pad[pl.ds(0, REACH)] = zeros[:, :width]
    gelu_pad[pl.ds(REACH + length, REACH)] = zeros[:, :width]
    for copy in kept:
        copy.wait()

    def project(s):
        at = span(s)
        wide = saved_all[at].astype(F32)
        inverse = lax.rsqrt(jnp.mean(wide * wide, axis=-1, keepdims=True) + EPSILON)
        block = (wide * inverse).astype(BF16)
        normed[at] = block
        for j in range(3):
            proj[j, at] = dot(block, w_qkv[j], NT).astype(BF16)

    def project_all(*offsets):
        for offset in offsets:
            project(seq_at(*offset))

    get_saved[0][1]()
    project_all((0, 0))
    get_saved[1][1]()
    get_upstream[0][0]()
    get_upstream[1][0]()
    get_weight[1]()
    project_all((3, 0))
    get_saved[0][2]()
    project_all((1, 0))
    get_saved[1][2]()
    get_weight[2]()
    project_all((0, 1))
    get_upstream[0][1]()
    get_saved[0][3]()
    get_saved[1][3]()
    project_all((1, 1))
    get_upstream[1][1]()
    get_weight[3]()
    swapped = []
    for offset in SEQ_OFFSETS:
        to = seq_at(*offset)
        swapped.append(wires.send(attn_blocks.at[to], attn_all.at[span(here)], {"seq": to}))
    attn_all[span(here)] = attn_blocks[here]
    gelu_pad[span(here, base=REACH)] = gelu_out_blocks[here]
    project_all((2, 0), (3, 1))
    get_upstream[0][2]()
    project_all((2, 1))
    get_upstream[1][2]()
    get_weight[4]()

    tile = 256
    sums[...] = jnp.zeros_like(sums)

    @pl.loop(0, length // tile)
    def _(index):
        at = pl.ds(pl.multiple_of(index * tile, tile), tile)
        weight = jnp.exp(dot(proj[1, at], proj[0], NT) * scale)
        expo[at] = weight
        sums[...] += jnp.sum(weight, axis=0, keepdims=True)

    def attend(s):
        at = span(s)
        grad_attn[at] = dot(upstream_all[at], w_out[...], NT).astype(BF16)

    def attend_all(*offsets):
        for offset in offsets:
            attend(seq_at(*offset))

    attend_all((0, 0), (3, 0), (1, 0), (0, 1))
    get_weight[5]()
    get_upstream[0][3]()
    get_upstream[1][3]()
    attend_all((1, 1), (2, 0), (3, 1), (2, 1))
    gelu_swapped = []
    for offset in SEQ_OFFSETS:
        to = seq_at(*offset)
        gelu_swapped.append(
            wires.send(gelu_out_blocks.at[to], gelu_pad.at[span(here, base=REACH)], {"seq": to})
        )
    for copy in swapped:
        copy.wait_recv()

    product = grad_attn[...].astype(F32) * attn_all[...].astype(F32)
    delta = lax.dot_general(
        jnp.ones((8, width), F32), product, (NT, ((), ())),
        precision=lax.Precision.HIGHEST, preferred_element_type=F32,
    )[0:1]
    ratio = 1.0 / sums[...]
    query_acc[...] = jnp.zeros_like(query_acc)

    @pl.loop(0, length // tile)
    def _(index):
        at = pl.ds(pl.multiple_of(index * tile, tile), tile)
        probs = expo[at] * ratio
        grad_prob = dot(proj[2, at], grad_attn[...], NT)
        score = (probs * (grad_prob - delta) * scale).astype(BF16)
        grad_proj[1, at] = dot(score, proj[0], NN).astype(BF16)
        grad_proj[2, at] = dot(probs.astype(BF16), grad_attn[...], NN).astype(BF16)
        query_acc[...] += dot(score, proj[1, at], TN)

    grad_proj[0] = query_acc[...].astype(BF16)

    def acts(s):
        at = span(s)

        @pl.loop(0, channels // 512)
        def _(index):
            columns = pl.ds(pl.multiple_of(index * 512, 512), 512)
            total = dot(grad_proj[0, at], w_qkv[0, :, columns], NN)
            total += dot(grad_proj[1, at], w_qkv[1, :, columns], NN)
            total += dot(grad_proj[2, at], w_qkv[2, :, columns], NN)
            parts[s, :, columns] = total.astype(BF16)

    scatter = [scatter_steps(wires, parts, inbox, part * half_rows, half_rows) for part in range(2)]

    def both(step):
        for steps in scatter:
            steps[step]()

    acts(seq_at(2, 1))
    both(0)
    acts(seq_at(3, 1))
    both(1)
    acts(seq_at(2, 0))
    both(2)
    acts(seq_at(1, 1))
    acts(seq_at(0, 1))
    both(3)
    acts(seq_at(3, 0))
    acts(seq_at(1, 0))
    both(4)
    acts(seq_at(0, 0))
    both(5)

    sum_qkv = total_steps(wires, qkv_terms, q0, q1, q2, q3, qkv_sum)
    sum_out = total_steps(wires, out_terms, o0, o1, o2, o3, out_sum)

    def seq_qkv(first):
        @pl.loop(first, first + 2)
        def _(index):
            columns = pl.ds(pl.multiple_of(index * 384, 384), 384)
            turned = normed[:, columns].T
            for j in range(3):
                result = dot(turned, grad_proj[j], NN).astype(BF16)
                qkv_terms[pl.ds(index * 4, 4), :, pl.ds(j * 48, 48)] = result.reshape(
                    4, 2, 48, width
                )

    seq_qkv(0)
    scatter[0][6]()
    seq_qkv(2)
    scatter[1][6]()
    sum_qkv[0]()
    slot_of, column_of = iotas((512, width))
    for part in range(2):
        pick = one_hot(slot_of, column_of, 6, 16, 6 * part)
        gelu_wide[pl.ds(512 * part, 512)] = dot(pick, attn_all[...], NT).astype(BF16)

    @pl.loop(0, 3)
    def _(index):
        first = dot(
            gelu_wide[pl.ds(0, 512)],
            upstream_all[:, pl.ds(pl.multiple_of(index * 256, 256), 256)],
            NN,
        )
        second = dot(
            gelu_wide[pl.ds(512, 512)],
            upstream_all[:, pl.ds(pl.multiple_of(half + index * 256, 256), 256)],
            NN,
        )
        result = (first + second).astype(BF16).reshape(16, 2, 16, 256)
        out_terms[:, :, :, pl.ds(pl.multiple_of(index * 256, 256), 256)] = result

    sum_out[0]()
    sum_qkv[1]()
    at_mine = span(here, base=REACH)
    for part in range(2):
        acts_here = scatter[part][7]()
        at = pl.ds(part * half_rows, half_rows)
        wide = saved[at].astype(F32)
        inverse = lax.rsqrt(jnp.mean(wide * wide, axis=-1, keepdims=True) + EPSILON)
        straight = wide * inverse
        grad = inverse * (
            acts_here - straight * jnp.mean(acts_here * straight, axis=-1, keepdims=True)
        )
        mid_pad[span(here, part * half_rows, half_rows, REACH)] = (
            upstream[at].astype(F32) + grad
        ).astype(BF16)
        get_mid[part][0]()
    sum_out[1]()
    sum_qkv[2]()
    sum_out[2]()

    for copy in gelu_swapped:
        copy.wait_recv()
    slot_of, column_of = iotas((tile, width))

    @pl.loop(0, 4)
    def _(index):
        total = jnp.zeros((tile, length), F32)
        for tap in range(TAPS):
            pick = one_hot(slot_of + index * tile, column_of, 6, 32, 6 * tap)
            total += dot(pick, gelu_pad[pl.ds(DILATION * tap, length)], NT)
        gelu_wide[pl.ds(pl.multiple_of(index * tile, tile), tile)] = total.astype(BF16)

    get_mid[0][1]()
    get_mid[1][1]()
    sum_qkv[3]()
    sum_out[3]()

    get_weight[6]()
    row_of, slot_of = iotas((width, length))

    def taps_of(first, last):
        for tap in range(first, last):
            pick = one_hot(ring_slot(slot_of), row_of, 6, 32, 6 * tap)

            @pl.loop(0, 3)
            def _(index):
                columns = pl.ds(pl.multiple_of(index * 512, 512), 512)
                weight = blocks[:, :, :, :, columns].reshape(length, 512)
                w_taps[tap, :, columns] = dot(pick, weight, NN).astype(BF16)

    taps_of(0, 3)
    get_mid[0][2]()
    sum_qkv[4]()
    sum_out[4]()
    taps_of(3, TAPS)
    get_mid[1][2]()
    for step in (5, 6):
        sum_qkv[step]()
        sum_out[step]()
    get_mid[0][3]()
    get_mid[1][3]()

    totals = [
        total_steps(wires, conv_a, a0, a1, a2, a3, conv_sum_a),
        total_steps(wires, conv_b, b0, b1, b2, b3, conv_sum_b),
    ]
    for part, terms in enumerate((conv_a, conv_b)):

        @pl.loop(0, 4)
        def _(index):
            at = pl.ds(pl.multiple_of(index * tile, tile), tile)
            for column in range(0, half, 256):
                result = dot(
                    gelu_wide[at],
                    mid_pad[pl.ds(REACH, length), pl.ds(part * half + column, 256)],
                    NN,
                ).astype(BF16)
                terms[pl.ds(index * 4, 4), :, :, pl.ds(column, 256)] = result.reshape(4, 2, 32, 256)

        totals[part][0]()

    def grad_gelu(first):
        @pl.loop(first, first + 2)
        def _(index):
            total = jnp.zeros((tile, width), F32)
            for tap in range(TAPS):
                at = pl.ds(pl.multiple_of(index * tile + (2 * REACH - DILATION * tap), 32), tile)
                total += dot(mid_pad[at], w_taps[tap], NT)
            gelu_send[pl.ds(index * 2, 2)] = total.astype(BF16).reshape(2, rows, width)

    totals[0][1]()
    grad_gelu(0)
    totals[1][1]()
    totals[0][2]()
    grad_gelu(2)
    totals[1][2]()
    swapped = []
    for offset in SEQ_OFFSETS:
        to = seq_at(*offset)
        swapped.append(wires.send(gelu_send.at[to], gelu_back.at[here], {"seq": to}))
    gelu_back[here] = gelu_send[here]
    for step in range(3, 5):
        for steps in totals:
            steps[step]()
    for copy in swapped:
        copy.wait_recv()
    for index in range(4):
        columns = pl.ds(index * pair, pair)
        gelu_grad = dot(gelu_back[2 * index], picks[0], NT) + dot(
            gelu_back[2 * index + 1], picks[1], NT
        )
        grad_rows[:, columns] = (
            mid_pad[at_mine, columns].astype(F32) + slope[:, columns] * gelu_grad
        ).astype(BF16)
    for step in range(5, 7):
        for steps in totals:
            steps[step]()
    wires.finish()


def run(inputs, saved, attn, upstream, w_qkv, w_out, w_block):
    rows, channels = saved.shape
    length, width, half = 8 * rows, w_out.shape[0], channels // 2
    count = 2 * (3 * GATHER_SENDS + SCATTER_SENDS) + WEIGHT_SENDS + 3 * 7 + 4 * TOTAL_SENDS
    in_vmem = pl.BlockSpec(memory_space=VMEM)
    return pl.pallas_call(
        kernel,
        out_shape=[
            jax.ShapeDtypeStruct((rows, channels), BF16),
            jax.ShapeDtypeStruct((144, width), BF16),
            jax.ShapeDtypeStruct((16, half), BF16),
            jax.ShapeDtypeStruct((32, half), BF16),
            jax.ShapeDtypeStruct((32, half), BF16),
        ],
        in_specs=[in_vmem] * 7,
        out_specs=[in_vmem] * 5,
        scratch_shapes=[
            VMEM((length, channels), BF16),
            VMEM((length, channels), BF16),
            VMEM((length + 2 * REACH, channels), BF16),
            VMEM((length + 2 * REACH, width), BF16),
            VMEM((length, width), BF16),
            VMEM((8, rows, width), BF16),
            VMEM((8, rows, width), BF16),
            VMEM((rows, channels), F32),
            VMEM((8, 2, 2, 32, channels), BF16),
            VMEM((length, channels), BF16),
            VMEM((3, length, width), BF16),
            VMEM((length, length), F32),
            VMEM((1, length), F32),
            VMEM((length, width), BF16),
            VMEM((length, width), F32),
            VMEM((3, length, width), BF16),
            VMEM((8, rows, channels), BF16),
            VMEM((7, rows, channels), BF16),
            VMEM((16, 2, 144, width), BF16),
            VMEM((16, 2, 16, half), BF16),
            VMEM((length, length), BF16),
            VMEM((TAPS, width, channels), BF16),
            VMEM((16, 2, 32, half), BF16),
            VMEM((16, 2, 32, half), BF16),
            VMEM((8, rows, width), BF16),
            VMEM((8, rows, width), BF16),
        ]
        + total_scratch(144, width)
        + total_scratch(16, half)
        + total_scratch(32, half)
        + total_scratch(32, half)
        + sems(count)
        + [pltpu.SemaphoreType.DMA((3,))],
        compiler_params=pltpu.CompilerParams(
            collective_id=1, has_side_effects=True, vmem_limit_bytes=58 << 20
        ),
    )(inputs, saved, attn, upstream, w_qkv, w_out, w_block)


def local(inputs, saved, attn_saved, upstream, w_qkv, w_out, w_conv):
    channels = inputs.shape[2]
    width = w_out.shape[0]
    taps_rows = w_conv.shape[0] * w_conv.shape[1]
    w_block = jnp.pad(w_conv.reshape(taps_rows, channels), ((0, 32 - taps_rows), (0, 0)))
    grad_rows, qkv_sum, out_sum, sum_a, sum_b = run(
        inputs[0], saved[0], attn_saved[0], upstream[0], w_qkv.transpose(1, 2, 0), w_out, w_block
    )
    out_pair = out_sum[:12].reshape(2, 6, channels // 2)
    return (
        grad_rows[None],
        qkv_sum.reshape(3, channels // 32, width).transpose(1, 0, 2),
        jnp.concatenate([out_pair[0], out_pair[1]], axis=1),
        jnp.concatenate([sum_a, sum_b], axis=1)[:taps_rows].reshape(w_conv.shape),
    )


def solution(mesh):
    placed = (
        P("dp", "seq", None),
        P("dp", "seq", None),
        P("dp", "seq", None),
        P("dp", "seq", None),
        P(None, None, "seq"),
        P("seq", None),
        P(None, ("seq", "dp"), None),
    )
    return jax.shard_map(
        local,
        mesh=mesh,
        in_specs=placed,
        out_specs=(
            P("dp", "seq", None),
            P("dp", None, "seq"),
            P(("seq", "dp"), None),
            P(None, ("seq", "dp"), None),
        ),
        check_vma=False,
    )
```

```python
import math

import jax
import jax.numpy as jnp
from jax import lax
from jax.experimental import pallas as pl
from jax.experimental.pallas import tpu as pltpu
from jax.sharding import PartitionSpec as P

HD = 192
TAPS = 5
DILATION = 32
EPSILON = 1e-06
REACH = DILATION * (TAPS // 2)
BF16 = jnp.bfloat16
F32 = jnp.float32
MESH = pl.DeviceIdType.MESH
VMEM = pltpu.VMEM
ANY = pl.ANY


def seq_at(dy, dx):
    here = lax.axis_index("seq")
    return lax.rem(here // 2 + dy, 4) * 2 + lax.rem(here + dx, 2)


def dp_at(dxh, dz, dcore):
    here = lax.axis_index("dp")
    core = lax.rem(here + dcore, 2)
    z = lax.rem(here // 2 + dz, 8)
    xh = lax.rem(here // 16 + dxh, 2)
    return (xh * 8 + z) * 2 + core


SEQ_OFFSETS = [(dy, dx) for dy in (2, 1, 3, 0) for dx in (1, 0) if (dy, dx) != (0, 0)]


def meet(peers):
    barrier = pltpu.get_barrier_semaphore()
    for peer in peers:
        pl.semaphore_signal(barrier, inc=1, device_id=peer, device_id_type=MESH)
    pl.semaphore_wait(barrier, len(peers))


class Wires:
    def __init__(self, send_sems, recv_sems):
        self.send_sems, self.recv_sems = send_sems, recv_sems
        self.used = 0
        self.copies = []

    def send(self, source, target, device):
        copy = pltpu.make_async_remote_copy(
            source,
            target,
            self.send_sems.at[self.used],
            self.recv_sems.at[self.used],
            device_id=device,
            device_id_type=MESH,
        )
        copy.start()
        self.used += 1
        self.copies.append(copy)
        return copy

    def finish(self):
        for copy in self.copies:
            copy.wait_send()


def gather_steps(wires, source, whole, base, rows):
    def place(s, start, count):
        return whole(s, base + start, count)

    up, down, across = {"seq": seq_at(1, 0)}, {"seq": seq_at(3, 0)}, {"seq": seq_at(0, 1)}
    half = rows // 2
    state = {}

    def first():
        mine = place(lax.axis_index("seq"), 0, rows)
        state["up"] = wires.send(source, mine, up)
        state["down"] = wires.send(source, mine, down)
        state["across"] = wires.send(source, mine, across)

    def second():
        state["up"].wait_recv()
        part = place(seq_at(3, 0), 0, half)
        state["far_up"] = wires.send(part, part, up)
        state["down"].wait_recv()
        part = place(seq_at(1, 0), half, half)
        state["far_down"] = wires.send(part, part, down)
        part = place(seq_at(1, 0), 0, rows)
        state["over"] = wires.send(part, part, across)
        state["across"].wait_recv()
        part = place(seq_at(0, 1), 0, rows)
        state["side_up"] = wires.send(part, part, up)

    def third():
        state["over"].wait_recv()
        part = place(seq_at(1, 1), 0, rows)
        state["side_down"] = wires.send(part, part, down)

    def last():
        for name in ("far_up", "far_down", "side_up", "side_down"):
            state[name].wait_recv()

    return first, second, third, last


GATHER_SENDS = 8


def scatter_steps(wires, parts, inbox, base, rows):
    up, down, across = {"seq": seq_at(1, 0)}, {"seq": seq_at(3, 0)}, {"seq": seq_at(0, 1)}
    here = lax.axis_index("seq")
    every = pl.ds(base, rows)
    top, bottom = pl.ds(base, rows // 2), pl.ds(base + rows // 2, rows // 2)
    state = {}

    def post(name, source, target, device):
        state[name] = wires.send(source, target, device)

    def far_side_up():
        post("c1", parts.at[seq_at(2, 1), every], inbox.at[0, every], up)

    def far_side_down():
        post("c2", parts.at[seq_at(3, 1), every], inbox.at[1, every], down)

    def far():
        post("ct", parts.at[seq_at(2, 0), top], inbox.at[2, top], down)
        post("cb", parts.at[seq_at(2, 0), bottom], inbox.at[2, bottom], up)

    def across_first():
        state["c1"].wait_recv()
        inbox[0, every] = inbox[0, every] + parts[seq_at(1, 1), every]
        post("c4", inbox.at[0, every], inbox.at[3, every], across)

    def across_second():
        state["c2"].wait_recv()
        inbox[1, every] = inbox[1, every] + parts[seq_at(0, 1), every]
        post("c5", inbox.at[1, every], inbox.at[4, every], across)

    def near_down():
        to = seq_at(3, 0)
        post("c6b", parts.at[to, bottom], inbox.at[5, bottom], down)
        state["ct"].wait_recv()
        inbox[2, top] = inbox[2, top] + parts[to, top]
        post("c6t", inbox.at[2, top], inbox.at[5, top], down)

    def near_up():
        state["cb"].wait_recv()
        state["c4"].wait_recv()
        to = seq_at(1, 0)
        inbox[3, every] = (parts[to, every].astype(F32) + inbox[3, every].astype(F32)).astype(BF16)
        inbox[3, bottom] = inbox[3, bottom] + inbox[2, bottom]
        post("c7", inbox.at[3, every], inbox.at[6, every], up)

    def last():
        for name in ("c5", "c6b", "c6t", "c7"):
            state[name].wait_recv()
        return (parts[here, every].astype(F32) + inbox[4, every].astype(F32)) + (
            inbox[5, every].astype(F32) + inbox[6, every].astype(F32)
        )

    return far_side_up, far_side_down, far, across_first, across_second, near_down, near_up, last


SCATTER_SENDS = 9


def total_steps(wires, terms, acc, above, below, beside, write):
    core = lax.rem(lax.axis_index("dp"), 2)
    z = lax.rem(lax.axis_index("dp") // 2, 8)
    xh = lax.axis_index("dp") // 16
    twin, up, down = {"dp": dp_at(0, 0, 1)}, {"dp": dp_at(0, 1, 0)}, {"dp": dp_at(0, 7, 0)}
    far = {"dp": dp_at(1, 0, 0)}
    state = {}

    def at(dz):
        return lax.rem(z + dz, 8)

    def start():
        state["twin"] = wires.send(terms.at[:, 1 - core], acc, twin)

    def first():
        state["twin"].wait_recv()
        chips = terms.shape[0]

        @pl.loop(0, chips)
        def _(chip):
            acc[chip] = acc[chip] + terms[chip, core]

        state["u"] = wires.send(acc.at[at(4)], above.at[0, 0], up)
        state["d"] = wires.send(acc.at[8 + at(4)], below.at[0, 1], down)

    def middle(step):
        def run():
            to_up, to_down = at(4 - step), at(4 + step)
            state["u"].wait_recv()
            acc[to_up] = acc[to_up] + above[step - 1, 0]
            if step > 1:
                acc[8 + to_up] = acc[8 + to_up] + above[step - 1, 1]
            state["u0"] = wires.send(acc.at[to_up], above.at[step, 0], up)
            state["u1"] = wires.send(acc.at[8 + to_up], above.at[step, 1], up)
            state["d"].wait_recv()
            acc[8 + to_down] = acc[8 + to_down] + below[step - 1, 1]
            if step > 1:
                acc[to_down] = acc[to_down] + below[step - 1, 0]
            state["d0"] = wires.send(acc.at[to_down], below.at[step, 0], down)
            state["d1"] = wires.send(acc.at[8 + to_down], below.at[step, 1], down)
            state["u"], state["d"] = Both(state["u0"], state["u1"]), Both(state["d0"], state["d1"])

        return run

    def cross():
        state["u"].wait_recv()
        state["d"].wait_recv()
        other = 1 - xh
        to = other * 8 + z
        acc[to] = (
            acc[to].astype(F32) + above[3, other].astype(F32) + below[3, other].astype(F32)
        ).astype(BF16)
        state["far"] = wires.send(acc.at[to], beside, far)

    def last():
        state["far"].wait_recv()
        total = acc[xh * 8 + z].astype(F32) + above[3, xh].astype(F32)
        write(total + below[3, xh].astype(F32) + beside[...].astype(F32))

    return start, first, middle(1), middle(2), middle(3), cross, last


TOTAL_SENDS = 1 + 2 + 3 * 4 + 1


class Both:
    def __init__(self, *copies):
        self.copies = copies

    def wait_recv(self):
        for copy in self.copies:
            copy.wait_recv()


def total_scratch(rows, columns):
    return [
        VMEM((16, rows, columns), BF16),
        VMEM((4, 2, rows, columns), BF16),
        VMEM((4, 2, rows, columns), BF16),
        VMEM((rows, columns), BF16),
    ]


def sems(count):
    return [pltpu.SemaphoreType.DMA((count,)), pltpu.SemaphoreType.DMA((count,))]


def weight_steps(wires, block, blocks):
    core = lax.rem(lax.axis_index("dp"), 2)
    z = lax.rem(lax.axis_index("dp") // 2, 8)
    xh = lax.axis_index("dp") // 16
    twin, up, down = {"dp": dp_at(0, 0, 1)}, {"dp": dp_at(0, 1, 0)}, {"dp": dp_at(0, 7, 0)}
    far = {"dp": dp_at(1, 0, 0)}
    state = {}

    def at(dz):
        return lax.rem(z + dz, 8)

    def start():
        state["far"] = wires.send(block, blocks.at[z, xh, core], far)

    def pass_on(step):
        def run():
            if step == 0:
                state["far"].wait_recv()
            else:
                state["up"].wait_recv()
                state["down"].wait_recv()
            low, high = at(8 - step), at(step)
            if step < 3:
                above, below = blocks.at[low, :, core], blocks.at[high, :, core]
            else:
                above, below = blocks.at[low, 0, core], blocks.at[high, 1, core]
            state["up"] = wires.send(above, above, up)
            state["down"] = wires.send(below, below, down)

        return run

    def share():
        state["up"].wait_recv()
        state["down"].wait_recv()
        part = blocks.at[:, :, core]
        state["twin"] = wires.send(part, part, twin)

    def last():
        state["twin"].wait_recv()

    return start, pass_on(0), pass_on(1), pass_on(2), pass_on(3), share, last


WEIGHT_SENDS = 1 + 8 + 1


def iotas(shape):
    return lax.broadcasted_iota(jnp.int32, shape, 0), lax.broadcasted_iota(jnp.int32, shape, 1)


def one_hot(slot, column, group, slots, offset):
    shift = slots.bit_length() - 1
    device, inside = lax.shift_right_logical(slot, shift), lax.bitwise_and(slot, slots - 1)
    within = jnp.logical_and(inside >= offset, inside < offset + group)
    hit = jnp.logical_and(device * group + inside - offset == column, within)
    return jnp.where(hit, 1.0, 0.0).astype(BF16)


def ring_slot(slot):
    z = lax.shift_right_logical(slot, 7)
    xh = lax.bitwise_and(lax.shift_right_logical(slot, 6), 1)
    return xh * 512 + z * 64 + lax.bitwise_and(slot, 63)


def dot(a, b, dims):
    return lax.dot_general(a, b, (dims, ((), ())), preferred_element_type=F32)


NN, NT, TN = ((1,), (0,)), ((1,), (1,)), ((0,), (0,))


def kernel(
    inputs, saved, attn, upstream, w_qkv, w_out, w_conv,
    grad_rows, qkv_sum, grad_out, grad_conv,
    w_block,
    saved_all, upstream_all, mid_pad, gelu_pad, attn_all, gelu_out_blocks, attn_blocks, slope,
    blocks, normed, proj, expo, sums, grad_attn, query_acc, grad_proj, parts, inbox,
    qkv_terms, out_terms, gelu_wide, w_taps, conv_a, conv_b, gelu_send, gelu_back,
    q0, q1, q2, q3, o0, o1, o2, o3, a0, a1, a2, a3, b0, b1, b2, b3,
    send_sems, recv_sems, own_sems,
):
    here = lax.axis_index("seq")
    core = lax.rem(lax.axis_index("dp"), 2)
    z = lax.rem(lax.axis_index("dp") // 2, 8)
    xh = lax.axis_index("dp") // 16
    rows, channels = saved.shape
    length = 8 * rows
    width = w_out.shape[0]
    half = channels // 2
    scale = HD ** (-0.5)
    meet(
        [{"seq": seq_at(*offset)} for offset in SEQ_OFFSETS]
        + [{"dp": dp_at(*offset)} for offset in ((0, 0, 1), (0, 1, 0), (0, 7, 0), (1, 0, 0))]
    )
    wires = Wires(send_sems, recv_sems)

    def span(s, start=0, count=rows, base=0):
        return pl.ds(pl.multiple_of(s * rows + (base + start), 32), count)

    def place_of(ref, base=0):
        return lambda s, start, count: ref.at[span(s, start, count, base)]

    half_rows = rows // 2

    def halves(source, whole):
        return [
            gather_steps(wires, source(part * half_rows), whole, part * half_rows, half_rows)
            for part in range(2)
        ]

    def rows_of(ref):
        return lambda start: ref.at[pl.ds(start, half_rows)]

    get_saved = halves(rows_of(saved), place_of(saved_all))
    get_upstream = halves(rows_of(upstream), place_of(upstream_all))
    get_mid = halves(lambda start: mid_pad.at[span(here, start, half_rows, REACH)], place_of(mid_pad, REACH))
    get_weight = weight_steps(wires, w_block, blocks)
    get_saved[0][0]()
    get_saved[1][0]()
    taps_rows = [w_conv[tap].astype(F32) for tap in range(TAPS)]
    w_block[...] = jnp.concatenate(taps_rows + [jnp.zeros((2, channels), F32)]).astype(BF16)
    get_weight[0]()
    kept = [
        pltpu.make_async_copy(saved, saved_all.at[span(here)], own_sems.at[0]),
        pltpu.make_async_copy(upstream, upstream_all.at[span(here)], own_sems.at[1]),
        pltpu.make_async_copy(w_block, blocks.at[z, xh, core], own_sems.at[2]),
    ]
    for copy in kept:
        copy.start()

    pair = 2 * width
    row_of, column_of = iotas((pair, width))
    picks = [(row_of == column_of + part * width) for part in range(2)]
    picks = [jnp.where(pick, 1.0, 0.0).astype(BF16) for pick in picks]
    for index in range(4):
        columns = pl.ds(index * pair, pair)
        value = inputs[:, columns].astype(F32)
        cubic = value * value * 0.044715
        inner = math.sqrt(2.0 / math.pi) * value * (1.0 + cubic)
        bend = jnp.tanh(inner)
        gelu = (0.5 * value * (1.0 + bend)).astype(BF16)
        slope[:, columns] = 0.5 * (1.0 + bend) + 0.5 * value * (1.0 - bend * bend) * (
            math.sqrt(2.0 / math.pi) * (1.0 + 3.0 * cubic)
        )
        attn_pair = attn[:, columns]
        for part in range(2):
            gelu_out_blocks[2 * index + part] = dot(gelu, picks[part], NN).astype(BF16)
            attn_blocks[2 * index + part] = dot(attn_pair, picks[part], NN).astype(BF16)
    zeros = jnp.zeros((REACH, channels), BF16)
    mid_pad[pl.ds(0, REACH)] = zeros
    mid_pad[pl.ds(REACH + length, REACH)] = zeros
    gelu_pad[pl.ds(0, REACH)] = zeros[:, :width]
    gelu_pad[pl.ds(REACH + length, REACH)] = zeros[:, :width]
    for copy in kept:
        copy.wait()

    def project(s):
        at = span(s)
        wide = saved_all[at].astype(F32)
        inverse = lax.rsqrt(jnp.mean(wide * wide, axis=-1, keepdims=True) + EPSILON)
        block = (wide * inverse).astype(BF16)
        normed[at] = block
        for j in range(3):
            proj[j, at] = dot(block, w_qkv[j], NT).astype(BF16)

    def project_all(*offsets):
        for offset in offsets:
            project(seq_at(*offset))

    get_saved[0][1]()
    project_all((0, 0))
    get_saved[1][1]()
    get_upstream[0][0]()
    get_upstream[1][0]()
    get_weight[1]()
    project_all((3, 0))
    get_saved[0][2]()
    project_all((1, 0))
    get_saved[1][2]()
    get_weight[2]()
    project_all((0, 1))
    get_upstream[0][1]()
    get_saved[0][3]()
    get_saved[1][3]()
    project_all((1, 1))
    get_upstream[1][1]()
    get_weight[3]()
    swapped = []
    for offset in SEQ_OFFSETS:
        to = seq_at(*offset)
        swapped.append(wires.send(attn_blocks.at[to], attn_all.at[span(here)], {"seq": to}))
    attn_all[span(here)] = attn_blocks[here]
    gelu_pad[span(here, base=REACH)] = gelu_out_blocks[here]
    project_all((2, 0), (3, 1))
    get_upstream[0][2]()
    project_all((2, 1))
    get_upstream[1][2]()
    get_weight[4]()

    tile = 256
    sums[...] = jnp.zeros_like(sums)

    @pl.loop(0, length // tile)
    def _(index):
        at = pl.ds(pl.multiple_of(index * tile, tile), tile)
        weight = jnp.exp(dot(proj[1, at], proj[0], NT) * scale)
        expo[at] = weight
        sums[...] += jnp.sum(weight, axis=0, keepdims=True)

    def attend(s):
        at = span(s)
        grad_attn[at] = dot(upstream_all[at], w_out[...], NT).astype(BF16)

    def attend_all(*offsets):
        for offset in offsets:
            attend(seq_at(*offset))

    attend_all((0, 0), (3, 0), (1, 0), (0, 1))
    get_weight[5]()
    get_upstream[0][3]()
    get_upstream[1][3]()
    attend_all((1, 1), (2, 0), (3, 1), (2, 1))
    gelu_swapped = []
    for offset in SEQ_OFFSETS:
        to = seq_at(*offset)
        gelu_swapped.append(
            wires.send(gelu_out_blocks.at[to], gelu_pad.at[span(here, base=REACH)], {"seq": to})
        )
    for copy in swapped:
        copy.wait_recv()

    product = grad_attn[...].astype(F32) * attn_all[...].astype(F32)
    delta = lax.dot_general(
        jnp.ones((8, width), F32), product, (NT, ((), ())),
        precision=lax.Precision.HIGHEST, preferred_element_type=F32,
    )[0:1]
    ratio = 1.0 / sums[...]
    query_acc[...] = jnp.zeros_like(query_acc)

    @pl.loop(0, length // tile)
    def _(index):
        at = pl.ds(pl.multiple_of(index * tile, tile), tile)
        probs = expo[at] * ratio
        grad_prob = dot(proj[2, at], grad_attn[...], NT)
        score = (probs * (grad_prob - delta) * scale).astype(BF16)
        grad_proj[1, at] = dot(score, proj[0], NN).astype(BF16)
        grad_proj[2, at] = dot(probs.astype(BF16), grad_attn[...], NN).astype(BF16)
        query_acc[...] += dot(score, proj[1, at], TN)

    grad_proj[0] = query_acc[...].astype(BF16)

    def acts(s):
        at = span(s)

        @pl.loop(0, channels // 512)
        def _(index):
            columns = pl.ds(pl.multiple_of(index * 512, 512), 512)
            total = dot(grad_proj[0, at], w_qkv[0, :, columns], NN)
            total += dot(grad_proj[1, at], w_qkv[1, :, columns], NN)
            total += dot(grad_proj[2, at], w_qkv[2, :, columns], NN)
            parts[s, :, columns] = total.astype(BF16)

    scatter = [scatter_steps(wires, parts, inbox, part * half_rows, half_rows) for part in range(2)]

    def both(step):
        for steps in scatter:
            steps[step]()

    acts(seq_at(2, 1))
    both(0)
    acts(seq_at(3, 1))
    both(1)
    acts(seq_at(2, 0))
    both(2)
    acts(seq_at(1, 1))
    acts(seq_at(0, 1))
    both(3)
    acts(seq_at(3, 0))
    acts(seq_at(1, 0))
    both(4)
    acts(seq_at(0, 0))
    both(5)

    def write_qkv(total):
        qkv_sum[...] = total.astype(BF16)

    def write_out(total):
        for part in range(2):
            grad_out[:, pl.ds(part * half, half)] = total[6 * part : 6 * part + 6].astype(BF16)

    def write_conv(part):
        def write(total):
            for tap in range(TAPS):
                rows_of_tap = total[6 * tap : 6 * tap + 6].astype(BF16)
                grad_conv[tap, :, pl.ds(part * half, half)] = rows_of_tap

        return write

    sum_qkv = total_steps(wires, qkv_terms, q0, q1, q2, q3, write_qkv)
    sum_out = total_steps(wires, out_terms, o0, o1, o2, o3, write_out)

    def seq_qkv(first):
        @pl.loop(first, first + 2)
        def _(index):
            columns = pl.ds(pl.multiple_of(index * 384, 384), 384)
            turned = normed[:, columns].T
            for j in range(3):
                result = dot(turned, grad_proj[j], NN).astype(BF16)
                qkv_terms[pl.ds(index * 4, 4), :, pl.ds(j * 48, 48)] = result.reshape(
                    4, 2, 48, width
                )

    seq_qkv(0)
    scatter[0][6]()
    seq_qkv(2)
    scatter[1][6]()
    sum_qkv[0]()
    slot_of, column_of = iotas((512, width))
    for part in range(2):
        pick = one_hot(slot_of, column_of, 6, 16, 6 * part)
        gelu_wide[pl.ds(512 * part, 512)] = dot(pick, attn_all[...], NT).astype(BF16)

    @pl.loop(0, 3)
    def _(index):
        first = dot(
            gelu_wide[pl.ds(0, 512)],
            upstream_all[:, pl.ds(pl.multiple_of(index * 256, 256), 256)],
            NN,
        )
        second = dot(
            gelu_wide[pl.ds(512, 512)],
            upstream_all[:, pl.ds(pl.multiple_of(half + index * 256, 256), 256)],
            NN,
        )
        result = (first + second).astype(BF16).reshape(16, 2, 16, 256)
        out_terms[:, :, :, pl.ds(pl.multiple_of(index * 256, 256), 256)] = result

    sum_out[0]()
    sum_qkv[1]()
    at_mine = span(here, base=REACH)
    for part in range(2):
        acts_here = scatter[part][7]()
        at = pl.ds(part * half_rows, half_rows)
        wide = saved[at].astype(F32)
        inverse = lax.rsqrt(jnp.mean(wide * wide, axis=-1, keepdims=True) + EPSILON)
        straight = wide * inverse
        grad = inverse * (
            acts_here - straight * jnp.mean(acts_here * straight, axis=-1, keepdims=True)
        )
        mid_pad[span(here, part * half_rows, half_rows, REACH)] = (
            upstream[at].astype(F32) + grad
        ).astype(BF16)
        get_mid[part][0]()
    sum_out[1]()
    sum_qkv[2]()
    sum_out[2]()

    for copy in gelu_swapped:
        copy.wait_recv()
    slot_of, column_of = iotas((tile, width))

    @pl.loop(0, 4)
    def _(index):
        total = jnp.zeros((tile, length), F32)
        for tap in range(TAPS):
            pick = one_hot(slot_of + index * tile, column_of, 6, 32, 6 * tap)
            total += dot(pick, gelu_pad[pl.ds(DILATION * tap, length)], NT)
        gelu_wide[pl.ds(pl.multiple_of(index * tile, tile), tile)] = total.astype(BF16)

    get_mid[0][1]()
    get_mid[1][1]()
    sum_qkv[3]()
    sum_out[3]()

    get_weight[6]()
    row_of, slot_of = iotas((width, length))

    def taps_of(first, last):
        for tap in range(first, last):
            pick = one_hot(ring_slot(slot_of), row_of, 6, 32, 6 * tap)

            @pl.loop(0, 3)
            def _(index):
                columns = pl.ds(pl.multiple_of(index * 512, 512), 512)
                weight = blocks[:, :, :, :, columns].reshape(length, 512)
                w_taps[tap, :, columns] = dot(pick, weight, NN).astype(BF16)

    taps_of(0, 3)
    get_mid[0][2]()
    sum_qkv[4]()
    sum_out[4]()
    taps_of(3, TAPS)
    get_mid[1][2]()
    for step in (5, 6):
        sum_qkv[step]()
        sum_out[step]()
    get_mid[0][3]()
    get_mid[1][3]()

    totals = [
        total_steps(wires, conv_a, a0, a1, a2, a3, write_conv(0)),
        total_steps(wires, conv_b, b0, b1, b2, b3, write_conv(1)),
    ]
    for part, terms in enumerate((conv_a, conv_b)):

        @pl.loop(0, 4)
        def _(index):
            at = pl.ds(pl.multiple_of(index * tile, tile), tile)
            for column in range(0, half, 256):
                result = dot(
                    gelu_wide[at],
                    mid_pad[pl.ds(REACH, length), pl.ds(part * half + column, 256)],
                    NN,
                ).astype(BF16)
                terms[pl.ds(index * 4, 4), :, :, pl.ds(column, 256)] = result.reshape(4, 2, 32, 256)

        totals[part][0]()

    def grad_gelu(first):
        @pl.loop(first, first + 2)
        def _(index):
            total = jnp.zeros((tile, width), F32)
            for tap in range(TAPS):
                at = pl.ds(pl.multiple_of(index * tile + (2 * REACH - DILATION * tap), 32), tile)
                total += dot(mid_pad[at], w_taps[tap], NT)
            gelu_send[pl.ds(index * 2, 2)] = total.astype(BF16).reshape(2, rows, width)

    totals[0][1]()
    grad_gelu(0)
    totals[1][1]()
    totals[0][2]()
    grad_gelu(2)
    totals[1][2]()
    swapped = []
    for offset in SEQ_OFFSETS:
        to = seq_at(*offset)
        swapped.append(wires.send(gelu_send.at[to], gelu_back.at[here], {"seq": to}))
    gelu_back[here] = gelu_send[here]
    for step in range(3, 5):
        for steps in totals:
            steps[step]()
    for copy in swapped:
        copy.wait_recv()
    for index in range(4):
        columns = pl.ds(index * pair, pair)
        gelu_grad = dot(gelu_back[2 * index], picks[0], NT) + dot(
            gelu_back[2 * index + 1], picks[1], NT
        )
        grad_rows[:, columns] = (
            mid_pad[at_mine, columns].astype(F32) + slope[:, columns] * gelu_grad
        ).astype(BF16)
    for step in range(5, 7):
        for steps in totals:
            steps[step]()
    wires.finish()


def run(inputs, saved, attn, upstream, w_qkv, w_out, w_conv):
    rows, channels = saved.shape
    length, width, half = 8 * rows, w_out.shape[0], channels // 2
    count = 2 * (3 * GATHER_SENDS + SCATTER_SENDS) + WEIGHT_SENDS + 3 * 7 + 4 * TOTAL_SENDS
    in_vmem = pl.BlockSpec(memory_space=VMEM)
    return pl.pallas_call(
        kernel,
        out_shape=[
            jax.ShapeDtypeStruct((rows, channels), BF16),
            jax.ShapeDtypeStruct((144, width), BF16),
            jax.ShapeDtypeStruct((6, channels), BF16),
            jax.ShapeDtypeStruct(w_conv.shape, BF16),
        ],
        in_specs=[in_vmem] * 7,
        out_specs=[in_vmem] * 4,
        scratch_shapes=[
            VMEM((32, channels), BF16),
            VMEM((length, channels), BF16),
            VMEM((length, channels), BF16),
            VMEM((length + 2 * REACH, channels), BF16),
            VMEM((length + 2 * REACH, width), BF16),
            VMEM((length, width), BF16),
            VMEM((8, rows, width), BF16),
            VMEM((8, rows, width), BF16),
            VMEM((rows, channels), F32),
            VMEM((8, 2, 2, 32, channels), BF16),
            VMEM((length, channels), BF16),
            VMEM((3, length, width), BF16),
            VMEM((length, length), F32),
            VMEM((1, length), F32),
            VMEM((length, width), BF16),
            VMEM((length, width), F32),
            VMEM((3, length, width), BF16),
            VMEM((8, rows, channels), BF16),
            VMEM((7, rows, channels), BF16),
            VMEM((16, 2, 144, width), BF16),
            VMEM((16, 2, 16, half), BF16),
            VMEM((length, length), BF16),
            VMEM((TAPS, width, channels), BF16),
            VMEM((16, 2, 32, half), BF16),
            VMEM((16, 2, 32, half), BF16),
            VMEM((8, rows, width), BF16),
            VMEM((8, rows, width), BF16),
        ]
        + total_scratch(144, width)
        + total_scratch(16, half)
        + total_scratch(32, half)
        + total_scratch(32, half)
        + sems(count)
        + [pltpu.SemaphoreType.DMA((3,))],
        compiler_params=pltpu.CompilerParams(
            collective_id=1, has_side_effects=True, vmem_limit_bytes=58 << 20
        ),
    )(inputs, saved, attn, upstream, w_qkv, w_out, w_conv)


def local(inputs, saved, attn_saved, upstream, w_qkv, w_out, w_conv):
    grad_rows, qkv_sum, grad_out, grad_conv = run(
        inputs[0], saved[0], attn_saved[0], upstream[0], w_qkv.transpose(1, 2, 0), w_out, w_conv
    )
    grad_qkv = qkv_sum.reshape(3, -1, w_out.shape[0]).transpose(1, 0, 2)
    return grad_rows[None], grad_qkv, grad_out, grad_conv


def solution(mesh):
    placed = (
        P("dp", "seq", None),
        P("dp", "seq", None),
        P("dp", "seq", None),
        P("dp", "seq", None),
        P(None, None, "seq"),
        P("seq", None),
        P(None, ("seq", "dp"), None),
    )
    return jax.shard_map(
        local,
        mesh=mesh,
        in_specs=placed,
        out_specs=(
            P("dp", "seq", None),
            P("dp", None, "seq"),
            P(("seq", "dp"), None),
            P(None, ("seq", "dp"), None),
        ),
        check_vma=False,
    )
```

```python
import math

import jax
import jax.numpy as jnp
from jax import lax
from jax.experimental import pallas as pl
from jax.experimental.pallas import tpu as pltpu
from jax.sharding import PartitionSpec as P

HD = 192
TAPS = 5
DILATION = 32
EPSILON = 1e-06
REACH = DILATION * (TAPS // 2)
BF16 = jnp.bfloat16
F32 = jnp.float32
MESH = pl.DeviceIdType.MESH
VMEM = pltpu.VMEM
ANY = pl.ANY


def seq_at(dy, dx):
    here = lax.axis_index("seq")
    return lax.rem(here // 2 + dy, 4) * 2 + lax.rem(here + dx, 2)


def dp_at(dxh, dz, dcore):
    here = lax.axis_index("dp")
    core = lax.rem(here + dcore, 2)
    z = lax.rem(here // 2 + dz, 8)
    xh = lax.rem(here // 16 + dxh, 2)
    return (xh * 8 + z) * 2 + core


SEQ_OFFSETS = [(dy, dx) for dy in (2, 1, 3, 0) for dx in (1, 0) if (dy, dx) != (0, 0)]


def meet(peers):
    barrier = pltpu.get_barrier_semaphore()
    for peer in peers:
        pl.semaphore_signal(barrier, inc=1, device_id=peer, device_id_type=MESH)
    pl.semaphore_wait(barrier, len(peers))


class Wires:
    def __init__(self, send_sems, recv_sems):
        self.send_sems, self.recv_sems = send_sems, recv_sems
        self.used = 0
        self.copies = []

    def send(self, source, target, device):
        copy = pltpu.make_async_remote_copy(
            source,
            target,
            self.send_sems.at[self.used],
            self.recv_sems.at[self.used],
            device_id=device,
            device_id_type=MESH,
        )
        copy.start()
        self.used += 1
        self.copies.append(copy)
        return copy

    def finish(self):
        for copy in self.copies:
            copy.wait_send()


def gather_steps(wires, source, whole, base, rows):
    def place(s, start, count):
        return whole(s, base + start, count)

    up, down, across = {"seq": seq_at(1, 0)}, {"seq": seq_at(3, 0)}, {"seq": seq_at(0, 1)}
    half = rows // 2
    state = {}

    def first():
        mine = place(lax.axis_index("seq"), 0, rows)
        state["up"] = wires.send(source, mine, up)
        state["down"] = wires.send(source, mine, down)
        state["across"] = wires.send(source, mine, across)

    def second():
        state["up"].wait_recv()
        part = place(seq_at(3, 0), 0, half)
        state["far_up"] = wires.send(part, part, up)
        state["down"].wait_recv()
        part = place(seq_at(1, 0), half, half)
        state["far_down"] = wires.send(part, part, down)
        part = place(seq_at(1, 0), 0, rows)
        state["over"] = wires.send(part, part, across)
        state["across"].wait_recv()
        part = place(seq_at(0, 1), 0, rows)
        state["side_up"] = wires.send(part, part, up)

    def third():
        state["over"].wait_recv()
        part = place(seq_at(1, 1), 0, rows)
        state["side_down"] = wires.send(part, part, down)

    def last():
        for name in ("far_up", "far_down", "side_up", "side_down"):
            state[name].wait_recv()

    return first, second, third, last


GATHER_SENDS = 8


def scatter_steps(wires, parts, inbox, base, rows):
    up, down, across = {"seq": seq_at(1, 0)}, {"seq": seq_at(3, 0)}, {"seq": seq_at(0, 1)}
    here = lax.axis_index("seq")
    every = pl.ds(base, rows)
    top, bottom = pl.ds(base, rows // 2), pl.ds(base + rows // 2, rows // 2)
    state = {}

    def post(name, source, target, device):
        state[name] = wires.send(source, target, device)

    def far_side_up():
        post("c1", parts.at[seq_at(2, 1), every], inbox.at[0, every], up)

    def far_side_down():
        post("c2", parts.at[seq_at(3, 1), every], inbox.at[1, every], down)

    def far():
        post("ct", parts.at[seq_at(2, 0), top], inbox.at[2, top], down)
        post("cb", parts.at[seq_at(2, 0), bottom], inbox.at[2, bottom], up)

    def across_first():
        state["c1"].wait_recv()
        inbox[0, every] = inbox[0, every] + parts[seq_at(1, 1), every]
        post("c4", inbox.at[0, every], inbox.at[3, every], across)

    def across_second():
        state["c2"].wait_recv()
        inbox[1, every] = inbox[1, every] + parts[seq_at(0, 1), every]
        post("c5", inbox.at[1, every], inbox.at[4, every], across)

    def near_down():
        to = seq_at(3, 0)
        post("c6b", parts.at[to, bottom], inbox.at[5, bottom], down)
        state["ct"].wait_recv()
        inbox[2, top] = inbox[2, top] + parts[to, top]
        post("c6t", inbox.at[2, top], inbox.at[5, top], down)

    def near_up():
        state["cb"].wait_recv()
        state["c4"].wait_recv()
        to = seq_at(1, 0)
        inbox[3, every] = (parts[to, every].astype(F32) + inbox[3, every].astype(F32)).astype(BF16)
        inbox[3, bottom] = inbox[3, bottom] + inbox[2, bottom]
        post("c7", inbox.at[3, every], inbox.at[6, every], up)

    def last():
        for name in ("c5", "c6b", "c6t", "c7"):
            state[name].wait_recv()
        return (parts[here, every].astype(F32) + inbox[4, every].astype(F32)) + (
            inbox[5, every].astype(F32) + inbox[6, every].astype(F32)
        )

    return far_side_up, far_side_down, far, across_first, across_second, near_down, near_up, last


SCATTER_SENDS = 9


def total_steps(wires, terms, acc, above, below, beside, write):
    core = lax.rem(lax.axis_index("dp"), 2)
    z = lax.rem(lax.axis_index("dp") // 2, 8)
    xh = lax.axis_index("dp") // 16
    twin, up, down = {"dp": dp_at(0, 0, 1)}, {"dp": dp_at(0, 1, 0)}, {"dp": dp_at(0, 7, 0)}
    far = {"dp": dp_at(1, 0, 0)}
    state = {}

    def at(dz):
        return lax.rem(z + dz, 8)

    def start():
        state["twin"] = wires.send(terms.at[:, 1 - core], acc, twin)

    def first():
        state["twin"].wait_recv()
        chips = terms.shape[0]

        @pl.loop(0, chips)
        def _(chip):
            acc[chip] = acc[chip] + terms[chip, core]

        state["u"] = wires.send(acc.at[at(4)], above.at[0, 0], up)
        state["d"] = wires.send(acc.at[8 + at(4)], below.at[0, 1], down)

    def middle(step):
        def run():
            to_up, to_down = at(4 - step), at(4 + step)
            state["u"].wait_recv()
            acc[to_up] = acc[to_up] + above[step - 1, 0]
            if step > 1:
                acc[8 + to_up] = acc[8 + to_up] + above[step - 1, 1]
            state["u0"] = wires.send(acc.at[to_up], above.at[step, 0], up)
            state["u1"] = wires.send(acc.at[8 + to_up], above.at[step, 1], up)
            state["d"].wait_recv()
            acc[8 + to_down] = acc[8 + to_down] + below[step - 1, 1]
            if step > 1:
                acc[to_down] = acc[to_down] + below[step - 1, 0]
            state["d0"] = wires.send(acc.at[to_down], below.at[step, 0], down)
            state["d1"] = wires.send(acc.at[8 + to_down], below.at[step, 1], down)
            state["u"], state["d"] = Both(state["u0"], state["u1"]), Both(state["d0"], state["d1"])

        return run

    def cross():
        state["u"].wait_recv()
        state["d"].wait_recv()
        other = 1 - xh
        to = other * 8 + z
        acc[to] = (
            acc[to].astype(F32) + above[3, other].astype(F32) + below[3, other].astype(F32)
        ).astype(BF16)
        state["far"] = wires.send(acc.at[to], beside, far)

    def last():
        state["far"].wait_recv()
        total = acc[xh * 8 + z].astype(F32) + above[3, xh].astype(F32)
        write(total + below[3, xh].astype(F32) + beside[...].astype(F32))

    return start, first, middle(1), middle(2), middle(3), cross, last


TOTAL_SENDS = 1 + 2 + 3 * 4 + 1


class Both:
    def __init__(self, *copies):
        self.copies = copies

    def wait_recv(self):
        for copy in self.copies:
            copy.wait_recv()


def total_scratch(rows, columns):
    return [
        VMEM((16, rows, columns), BF16),
        VMEM((4, 2, rows, columns), BF16),
        VMEM((4, 2, rows, columns), BF16),
        VMEM((rows, columns), BF16),
    ]


def sems(count):
    return [pltpu.SemaphoreType.DMA((count,)), pltpu.SemaphoreType.DMA((count,))]


def weight_steps(wires, block, blocks):
    core = lax.rem(lax.axis_index("dp"), 2)
    z = lax.rem(lax.axis_index("dp") // 2, 8)
    xh = lax.axis_index("dp") // 16
    twin, up, down = {"dp": dp_at(0, 0, 1)}, {"dp": dp_at(0, 1, 0)}, {"dp": dp_at(0, 7, 0)}
    far = {"dp": dp_at(1, 0, 0)}
    state = {}

    def at(dz):
        return lax.rem(z + dz, 8)

    def start():
        state["far"] = wires.send(block, blocks.at[z, xh, core], far)

    def pass_on(step):
        def run():
            if step == 0:
                state["far"].wait_recv()
            else:
                state["up"].wait_recv()
                state["down"].wait_recv()
            low, high = at(8 - step), at(step)
            if step < 3:
                above, below = blocks.at[low, :, core], blocks.at[high, :, core]
            else:
                above, below = blocks.at[low, 0, core], blocks.at[high, 1, core]
            state["up"] = wires.send(above, above, up)
            state["down"] = wires.send(below, below, down)

        return run

    def share():
        state["up"].wait_recv()
        state["down"].wait_recv()
        part = blocks.at[:, :, core]
        state["twin"] = wires.send(part, part, twin)

    def last():
        state["twin"].wait_recv()

    return start, pass_on(0), pass_on(1), pass_on(2), pass_on(3), share, last


WEIGHT_SENDS = 1 + 8 + 1


def iotas(shape):
    return lax.broadcasted_iota(jnp.int32, shape, 0), lax.broadcasted_iota(jnp.int32, shape, 1)


def one_hot(slot, column, group, slots, offset):
    shift = slots.bit_length() - 1
    device, inside = lax.shift_right_logical(slot, shift), lax.bitwise_and(slot, slots - 1)
    within = jnp.logical_and(inside >= offset, inside < offset + group)
    hit = jnp.logical_and(device * group + inside - offset == column, within)
    return jnp.where(hit, 1.0, 0.0).astype(BF16)


def ring_slot(slot):
    z = lax.shift_right_logical(slot, 7)
    xh = lax.bitwise_and(lax.shift_right_logical(slot, 6), 1)
    return xh * 512 + z * 64 + lax.bitwise_and(slot, 63)


def dot(a, b, dims):
    return lax.dot_general(a, b, (dims, ((), ())), preferred_element_type=F32)


NN, NT, TN = ((1,), (0,)), ((1,), (1,)), ((0,), (0,))


def kernel(
    inputs, saved, attn, upstream, w_qkv, w_out, w_conv,
    grad_rows, qkv_sum, grad_out, grad_conv,
    w_block,
    saved_all, upstream_all, mid_pad, gelu_pad, attn_all, gelu_out_blocks, attn_blocks, slope,
    blocks, normed, proj, expo, sums, grad_attn, query_acc, grad_proj, parts, inbox,
    qkv_terms, out_terms, gelu_wide, w_taps, conv_a, conv_b, gelu_send, gelu_back,
    q0, q1, q2, q3, o0, o1, o2, o3, a0, a1, a2, a3, b0, b1, b2, b3,
    send_sems, recv_sems, own_sems,
):
    here = lax.axis_index("seq")
    core = lax.rem(lax.axis_index("dp"), 2)
    z = lax.rem(lax.axis_index("dp") // 2, 8)
    xh = lax.axis_index("dp") // 16
    rows, channels = saved.shape
    length = 8 * rows
    width = w_out.shape[0]
    half = channels // 2
    scale = HD ** (-0.5)
    meet(
        [{"seq": seq_at(*offset)} for offset in SEQ_OFFSETS]
        + [{"dp": dp_at(*offset)} for offset in ((0, 0, 1), (0, 1, 0), (0, 7, 0), (1, 0, 0))]
    )
    wires = Wires(send_sems, recv_sems)

    def span(s, start=0, count=rows, base=0):
        return pl.ds(pl.multiple_of(s * rows + (base + start), 32), count)

    def place_of(ref, base=0):
        return lambda s, start, count: ref.at[span(s, start, count, base)]

    half_rows = rows // 2

    def halves(source, whole):
        return [
            gather_steps(wires, source(part * half_rows), whole, part * half_rows, half_rows)
            for part in range(2)
        ]

    def rows_of(ref):
        return lambda start: ref.at[pl.ds(start, half_rows)]

    get_saved = halves(rows_of(saved), place_of(saved_all))
    get_upstream = halves(rows_of(upstream), place_of(upstream_all))
    get_mid = halves(lambda start: mid_pad.at[span(here, start, half_rows, REACH)], place_of(mid_pad, REACH))
    get_weight = weight_steps(wires, w_block, blocks)
    get_saved[0][0]()
    get_saved[1][0]()
    taps_rows = [w_conv[tap].astype(F32) for tap in range(TAPS)]
    w_block[...] = jnp.concatenate(taps_rows + [jnp.zeros((2, channels), F32)]).astype(BF16)
    get_weight[0]()
    kept = [
        pltpu.make_async_copy(saved, saved_all.at[span(here)], own_sems.at[0]),
        pltpu.make_async_copy(upstream, upstream_all.at[span(here)], own_sems.at[1]),
        pltpu.make_async_copy(w_block, blocks.at[z, xh, core], own_sems.at[2]),
    ]
    for copy in kept:
        copy.start()

    pair = 2 * width
    row_of, column_of = iotas((pair, width))
    picks = [(row_of == column_of + part * width) for part in range(2)]
    picks = [jnp.where(pick, 1.0, 0.0).astype(BF16) for pick in picks]
    for index in range(4):
        columns = pl.ds(index * pair, pair)
        value = inputs[:, columns].astype(F32)
        cubic = value * value * 0.044715
        inner = math.sqrt(2.0 / math.pi) * value * (1.0 + cubic)
        bend = jnp.tanh(inner)
        gelu = (0.5 * value * (1.0 + bend)).astype(BF16)
        slope[:, columns] = 0.5 * (1.0 + bend) + 0.5 * value * (1.0 - bend * bend) * (
            math.sqrt(2.0 / math.pi) * (1.0 + 3.0 * cubic)
        )
        attn_pair = attn[:, columns]
        for part in range(2):
            gelu_out_blocks[2 * index + part] = dot(gelu, picks[part], NN).astype(BF16)
            attn_blocks[2 * index + part] = dot(attn_pair, picks[part], NN).astype(BF16)
    zeros = jnp.zeros((REACH, channels), BF16)
    mid_pad[pl.ds(0, REACH)] = zeros
    mid_pad[pl.ds(REACH + length, REACH)] = zeros
    gelu_pad[pl.ds(0, REACH)] = zeros[:, :width]
    gelu_pad[pl.ds(REACH + length, REACH)] = zeros[:, :width]
    for copy in kept:
        copy.wait()

    def project(s):
        at = span(s)
        wide = saved_all[at].astype(F32)
        inverse = lax.rsqrt(jnp.mean(wide * wide, axis=-1, keepdims=True) + EPSILON)
        block = (wide * inverse).astype(BF16)
        normed[at] = block
        for j in range(3):
            proj[j, at] = dot(block, w_qkv[j], NT).astype(BF16)

    def project_all(*offsets):
        for offset in offsets:
            project(seq_at(*offset))

    get_saved[0][1]()
    project_all((0, 0))
    get_saved[1][1]()
    get_upstream[0][0]()
    get_upstream[1][0]()
    get_weight[1]()
    project_all((3, 0))
    get_saved[0][2]()
    project_all((1, 0))
    get_saved[1][2]()
    get_weight[2]()
    project_all((0, 1))
    get_upstream[0][1]()
    get_saved[0][3]()
    get_saved[1][3]()
    project_all((1, 1))
    get_upstream[1][1]()
    get_weight[3]()
    swapped = []
    for offset in SEQ_OFFSETS:
        to = seq_at(*offset)
        swapped.append(wires.send(attn_blocks.at[to], attn_all.at[span(here)], {"seq": to}))
    attn_all[span(here)] = attn_blocks[here]
    gelu_pad[span(here, base=REACH)] = gelu_out_blocks[here]
    project_all((2, 0), (3, 1))
    get_upstream[0][2]()
    project_all((2, 1))
    get_upstream[1][2]()
    get_weight[4]()

    tile = 256
    sums[...] = jnp.zeros_like(sums)

    @pl.loop(0, length // tile)
    def _(index):
        at = pl.ds(pl.multiple_of(index * tile, tile), tile)
        weight = jnp.exp(dot(proj[1, at], proj[0], NT) * scale)
        expo[at] = weight
        sums[...] += jnp.sum(weight, axis=0, keepdims=True)

    def attend(s):
        at = span(s)
        grad_attn[at] = dot(upstream_all[at], w_out[...], NT).astype(BF16)

    def attend_all(*offsets):
        for offset in offsets:
            attend(seq_at(*offset))

    attend_all((0, 0), (3, 0), (1, 0), (0, 1))
    get_weight[5]()
    get_upstream[0][3]()
    get_upstream[1][3]()
    attend_all((1, 1), (2, 0), (3, 1), (2, 1))
    gelu_swapped = []
    for offset in SEQ_OFFSETS:
        to = seq_at(*offset)
        gelu_swapped.append(
            wires.send(gelu_out_blocks.at[to], gelu_pad.at[span(here, base=REACH)], {"seq": to})
        )
    for copy in swapped:
        copy.wait_recv()

    product = grad_attn[...].astype(F32) * attn_all[...].astype(F32)
    delta = lax.dot_general(
        jnp.ones((8, width), F32), product, (NT, ((), ())),
        precision=lax.Precision.HIGHEST, preferred_element_type=F32,
    )[0:1]
    ratio = 1.0 / sums[...]
    query_acc[...] = jnp.zeros_like(query_acc)

    @pl.loop(0, length // tile)
    def _(index):
        at = pl.ds(pl.multiple_of(index * tile, tile), tile)
        probs = expo[at] * ratio
        grad_prob = dot(proj[2, at], grad_attn[...], NT)
        score = (probs * (grad_prob - delta) * scale).astype(BF16)
        grad_proj[1, at] = dot(score, proj[0], NN).astype(BF16)
        grad_proj[2, at] = dot(probs.astype(BF16), grad_attn[...], NN).astype(BF16)
        query_acc[...] += dot(score, proj[1, at], TN)

    grad_proj[0] = query_acc[...].astype(BF16)

    def acts(s):
        at = span(s)

        @pl.loop(0, channels // 512)
        def _(index):
            columns = pl.ds(pl.multiple_of(index * 512, 512), 512)
            total = dot(grad_proj[0, at], w_qkv[0, :, columns], NN)
            total += dot(grad_proj[1, at], w_qkv[1, :, columns], NN)
            total += dot(grad_proj[2, at], w_qkv[2, :, columns], NN)
            parts[s, :, columns] = total.astype(BF16)

    scatter = [scatter_steps(wires, parts, inbox, part * half_rows, half_rows) for part in range(2)]

    def both(step):
        for steps in scatter:
            steps[step]()

    acts(seq_at(2, 1))
    both(0)
    acts(seq_at(3, 1))
    both(1)
    acts(seq_at(2, 0))
    both(2)
    acts(seq_at(1, 1))
    acts(seq_at(0, 1))
    both(3)
    acts(seq_at(3, 0))
    acts(seq_at(1, 0))
    both(4)
    acts(seq_at(0, 0))
    both(5)

    def write_qkv(total):
        qkv_sum[...] = total.astype(BF16)

    def write_out(total):
        for part in range(2):
            grad_out[:, pl.ds(part * half, half)] = total[6 * part : 6 * part + 6].astype(BF16)

    def write_conv(part):
        def write(total):
            for tap in range(TAPS):
                rows_of_tap = total[6 * tap : 6 * tap + 6].astype(BF16)
                grad_conv[tap, :, pl.ds(part * half, half)] = rows_of_tap

        return write

    sum_qkv = total_steps(wires, qkv_terms, q0, q1, q2, q3, write_qkv)
    sum_out = total_steps(wires, out_terms, o0, o1, o2, o3, write_out)

    def seq_qkv(first):
        @pl.loop(first, first + 2)
        def _(index):
            columns = pl.ds(pl.multiple_of(index * 384, 384), 384)
            turned = normed[:, columns].T
            for j in range(3):
                result = dot(turned, grad_proj[j], NN).astype(BF16)
                qkv_terms[pl.ds(index * 4, 4), :, pl.ds(j * 48, 48)] = result.reshape(
                    4, 2, 48, width
                )

    seq_qkv(0)
    scatter[0][6]()
    seq_qkv(2)
    scatter[1][6]()
    sum_qkv[0]()
    slot_of, column_of = iotas((512, width))
    for part in range(2):
        pick = one_hot(slot_of, column_of, 6, 16, 6 * part)
        gelu_wide[pl.ds(512 * part, 512)] = dot(pick, attn_all[...], NT).astype(BF16)

    @pl.loop(0, 3)
    def _(index):
        first = dot(
            gelu_wide[pl.ds(0, 512)],
            upstream_all[:, pl.ds(pl.multiple_of(index * 256, 256), 256)],
            NN,
        )
        second = dot(
            gelu_wide[pl.ds(512, 512)],
            upstream_all[:, pl.ds(pl.multiple_of(half + index * 256, 256), 256)],
            NN,
        )
        result = (first + second).astype(BF16).reshape(16, 2, 16, 256)
        out_terms[:, :, :, pl.ds(pl.multiple_of(index * 256, 256), 256)] = result

    sum_out[0]()
    sum_qkv[1]()
    at_mine = span(here, base=REACH)
    for part in range(2):
        acts_here = scatter[part][7]()
        at = pl.ds(part * half_rows, half_rows)
        wide = saved[at].astype(F32)
        inverse = lax.rsqrt(jnp.mean(wide * wide, axis=-1, keepdims=True) + EPSILON)
        straight = wide * inverse
        grad = inverse * (
            acts_here - straight * jnp.mean(acts_here * straight, axis=-1, keepdims=True)
        )
        mid_pad[span(here, part * half_rows, half_rows, REACH)] = (
            upstream[at].astype(F32) + grad
        ).astype(BF16)
        get_mid[part][0]()
    sum_out[1]()
    sum_qkv[2]()
    sum_out[2]()

    for copy in gelu_swapped:
        copy.wait_recv()
    slot_of, column_of = iotas((tile, width))

    @pl.loop(0, 4)
    def _(index):
        total = jnp.zeros((tile, length), F32)
        for tap in range(TAPS):
            pick = one_hot(slot_of + index * tile, column_of, 6, 32, 6 * tap)
            total += dot(pick, gelu_pad[pl.ds(DILATION * tap, length)], NT)
        gelu_wide[pl.ds(pl.multiple_of(index * tile, tile), tile)] = total.astype(BF16)

    get_mid[0][1]()
    get_mid[1][1]()
    sum_qkv[3]()
    sum_out[3]()

    get_weight[6]()
    row_of, slot_of = iotas((width, length))

    def taps_of(first, last):
        for tap in range(first, last):
            pick = one_hot(ring_slot(slot_of), row_of, 6, 32, 6 * tap)

            @pl.loop(0, 3)
            def _(index):
                columns = pl.ds(pl.multiple_of(index * 512, 512), 512)
                weight = blocks[:, :, :, :, columns].reshape(length, 512)
                w_taps[tap, :, columns] = dot(pick, weight, NN).astype(BF16)

    taps_of(0, 3)
    get_mid[0][2]()
    sum_qkv[4]()
    sum_out[4]()
    taps_of(3, TAPS)
    get_mid[1][2]()
    for step in (5, 6):
        sum_qkv[step]()
        sum_out[step]()
    get_mid[0][3]()
    get_mid[1][3]()

    totals = [
        total_steps(wires, conv_a, a0, a1, a2, a3, write_conv(0)),
        total_steps(wires, conv_b, b0, b1, b2, b3, write_conv(1)),
    ]
    for part, terms in enumerate((conv_a, conv_b)):

        @pl.loop(0, 4)
        def _(index):
            at = pl.ds(pl.multiple_of(index * tile, tile), tile)
            for column in range(0, half, 256):
                result = dot(
                    gelu_wide[at],
                    mid_pad[pl.ds(REACH, length), pl.ds(part * half + column, 256)],
                    NN,
                ).astype(BF16)
                terms[pl.ds(index * 4, 4), :, :, pl.ds(column, 256)] = result.reshape(4, 2, 32, 256)

        totals[part][0]()

    def grad_gelu(first):
        @pl.loop(first, first + 2)
        def _(index):
            total = jnp.zeros((tile, width), F32)
            for tap in range(TAPS):
                at = pl.ds(pl.multiple_of(index * tile + (2 * REACH - DILATION * tap), 32), tile)
                total += dot(mid_pad[at], w_taps[tap], NT)
            gelu_send[pl.ds(index * 2, 2)] = total.astype(BF16).reshape(2, rows, width)

    totals[0][1]()
    grad_gelu(0)
    totals[1][1]()
    totals[0][2]()
    grad_gelu(2)
    totals[1][2]()
    swapped = []
    for offset in SEQ_OFFSETS:
        to = seq_at(*offset)
        swapped.append(wires.send(gelu_send.at[to], gelu_back.at[here], {"seq": to}))
    gelu_back[here] = gelu_send[here]
    for step in range(3, 5):
        for steps in totals:
            steps[step]()
    for copy in swapped:
        copy.wait_recv()
    for index in range(4):
        columns = pl.ds(index * pair, pair)
        gelu_grad = dot(gelu_back[2 * index], picks[0], NT) + dot(
            gelu_back[2 * index + 1], picks[1], NT
        )
        grad_rows[:, columns] = (
            mid_pad[at_mine, columns].astype(F32) + slope[:, columns] * gelu_grad
        ).astype(BF16)
    for step in range(5, 7):
        for steps in totals:
            steps[step]()
    wires.finish()


def run(inputs, saved, attn, upstream, w_qkv, w_out, w_conv):
    rows, channels = saved.shape
    length, width, half = 8 * rows, w_out.shape[0], channels // 2
    count = 2 * (3 * GATHER_SENDS + SCATTER_SENDS) + WEIGHT_SENDS + 3 * 7 + 4 * TOTAL_SENDS
    in_vmem = pl.BlockSpec(memory_space=VMEM)
    return pl.pallas_call(
        kernel,
        out_shape=[
            jax.ShapeDtypeStruct((rows, channels), BF16),
            jax.ShapeDtypeStruct((144, width), BF16),
            jax.ShapeDtypeStruct((6, channels), BF16),
            jax.ShapeDtypeStruct(w_conv.shape, BF16),
        ],
        in_specs=[in_vmem] * 7,
        out_specs=[in_vmem] * 4,
        scratch_shapes=[
            VMEM((32, channels), BF16),
            VMEM((length, channels), BF16),
            VMEM((length, channels), BF16),
            VMEM((length + 2 * REACH, channels), BF16),
            VMEM((length + 2 * REACH, width), BF16),
            VMEM((length, width), BF16),
            VMEM((8, rows, width), BF16),
            VMEM((8, rows, width), BF16),
            VMEM((rows, channels), F32),
            VMEM((8, 2, 2, 32, channels), BF16),
            VMEM((length, channels), BF16),
            VMEM((3, length, width), BF16),
            VMEM((length, length), F32),
            VMEM((1, length), F32),
            VMEM((length, width), BF16),
            VMEM((length, width), F32),
            VMEM((3, length, width), BF16),
            VMEM((8, rows, channels), BF16),
            VMEM((7, rows, channels), BF16),
            VMEM((16, 2, 144, width), BF16),
            VMEM((16, 2, 16, half), BF16),
            VMEM((length, length), BF16),
            VMEM((TAPS, width, channels), BF16),
            VMEM((16, 2, 32, half), BF16),
            VMEM((16, 2, 32, half), BF16),
            VMEM((8, rows, width), BF16),
            VMEM((8, rows, width), BF16),
        ]
        + total_scratch(144, width)
        + total_scratch(16, half)
        + total_scratch(32, half)
        + total_scratch(32, half)
        + sems(count)
        + [pltpu.SemaphoreType.DMA((3,))],
        compiler_params=pltpu.CompilerParams(
            collective_id=1, has_side_effects=True, vmem_limit_bytes=58 << 20
        ),
    )(inputs, saved, attn, upstream, w_qkv, w_out, w_conv)


def hand_over_kernel(a, b, c, d, a_out, b_out, c_out, d_out, done):
    pairs = ((a, a_out), (b, b_out), (c, c_out), (d, d_out))
    copies = [pltpu.make_async_copy(*pair, done.at[i]) for i, pair in enumerate(pairs)]
    for copy in copies:
        copy.start()
    for copy in copies:
        copy.wait()


def hand_over(*results):
    anywhere = pl.BlockSpec(memory_space=ANY)
    return pl.pallas_call(
        hand_over_kernel,
        out_shape=[jax.ShapeDtypeStruct(result.shape, result.dtype) for result in results],
        in_specs=[pl.BlockSpec(memory_space=VMEM)] * 4,
        out_specs=[anywhere] * 4,
        scratch_shapes=[pltpu.SemaphoreType.DMA((4,))],
    )(*results)


def local(inputs, saved, attn_saved, upstream, w_qkv, w_out, w_conv):
    results = run(
        inputs[0], saved[0], attn_saved[0], upstream[0], w_qkv.transpose(1, 2, 0), w_out, w_conv
    )
    grad_rows, qkv_sum, grad_out, grad_conv = hand_over(*results)
    grad_qkv = qkv_sum.reshape(3, -1, w_out.shape[0]).transpose(1, 0, 2)
    return grad_rows[None], grad_qkv, grad_out, grad_conv


def solution(mesh):
    placed = (
        P("dp", "seq", None),
        P("dp", "seq", None),
        P("dp", "seq", None),
        P("dp", "seq", None),
        P(None, None, "seq"),
        P("seq", None),
        P(None, ("seq", "dp"), None),
    )
    return jax.shard_map(
        local,
        mesh=mesh,
        in_specs=placed,
        out_specs=(
            P("dp", "seq", None),
            P("dp", None, "seq"),
            P(("seq", "dp"), None),
            P(None, ("seq", "dp"), None),
        ),
        check_vma=False,
    )
```
